512 devices in a mesh: rep: 64 (over z, x), tp: 8 (over y, core).
Axes of the slice: x: 4, y: 4, z: 16, core: 2. Of those that a mesh axis runs over, the one named last changes fastest.
Arguments:
- first_hidden_rows: bfloat16 [8192, 3072], P('rep', 'tp'), may hold values from -40 to 40
- norm_scale: float32 [3072], P('tp'), may hold values from 0.1 to 1.9
- projection_weight: bfloat16 [3072, 3072], P('tp'), may hold values from -0.109375 to 0.109375
- down_weights: bfloat16 [256, 3072, 64], P('rep', 'tp'), may hold values from -0.109375 to 0.109375
- up_weights: bfloat16 [256, 64, 3072], P('rep', None, 'tp'), may hold values from -0.75 to 0.75
- requests: int32 [64, 64], replicated, may hold values from 0 to 255, as said below
Outputs:
- drafted: bfloat16 [2, 8192, 3072], P(None, 'rep', 'tp')
The draws below stay inside these ranges and needn't reach their ends.
Inputs may be any that keep to these rules, and one draw needn't show every extreme that they name: `requests`: adapter a is held by replica group a // 4. Each row g names adapters of every holding group, 1 entries for each of them.
All inputs are finite; a program needn't handle non-finite values.
Results may differ from the reference program's by a relative error of at most 0.019.
Values may be sent and summed in bfloat16 or wider, within the bound.
No kernel may reach another device: no remote copies, remote signals or barrier semaphores. Data moves between devices by JAX's collectives and lax.ppermute only.
A program may use at most 64 MiB of HBM per device.

```python
import jax
import jax.numpy as jnp
from jax import lax

MODEL_FEATURES = 3072
ADAPTER_RANK = 64
REQUEST_BLOCKS = 64
BLOCK_LENGTH = 2
AD_DEV = 4
DRAFT = 2
TOTAL_ROWS = 8192
ADAPTER_COUNT = 256
N_REP = 64
N_TP = 8


def draw_first_hidden_rows(key, part):
    key = jax.random.fold_in(key, 11)
    key_core, key_rows, key_rough = jax.random.split(key, 3)
    row_factor = 10.0 ** (jax.random.uniform(key_rows, (TOTAL_ROWS, 1), jnp.float32) - 1.0)
    column = jnp.arange(MODEL_FEATURES, dtype=jnp.float32) / MODEL_FEATURES
    rough = 2.0 ** jax.random.uniform(key_rough, (1, MODEL_FEATURES), jnp.float32)
    core = jax.random.truncated_normal(key_core, -4.0, 4.0, (TOTAL_ROWS, MODEL_FEATURES), jnp.float32)
    tilt = 3.0 ** column
    return (core * row_factor * tilt[None, :] * rough).astype(jnp.bfloat16)


def draw_requests(key, part):
    key = jax.random.fold_in(key, 23)
    group_keys = jax.random.split(key, N_REP)

    def group_list(group_key):
        key_order, key_local = jax.random.split(group_key, 2)
        holders = jnp.arange(N_REP, dtype=jnp.int32)
        listed = jax.random.permutation(key_order, jnp.repeat(holders, REQUEST_BLOCKS // N_REP))
        local_pick = jax.random.randint(key_local, (REQUEST_BLOCKS,), 0, AD_DEV)
        return (listed * AD_DEV + local_pick).astype(jnp.int32)
    return jax.vmap(group_list)(group_keys)


def shard_levels(key, dims, shards, least, top_value):
    level = 1.0
    for dim, shards_of in shards:
        heights = jax.random.uniform(jax.random.fold_in(jax.random.fold_in(key, 6), dim), (shards_of,), jnp.float32, least / len(shards), top_value / len(shards))
        level = level * jnp.repeat(jnp.exp(heights), dims[dim] // shards_of).reshape((-1,) + (1,) * (len(dims) - 1 - dim))
    return level


def noise(rng, dims, spread, limit, pieces=(), kind=jnp.bfloat16):
    result = spread * jax.random.normal(rng, dims, jnp.float32)
    if pieces:
        result = result * shard_levels(rng, dims, pieces, -0.22, 0.18)
    return jnp.clip(result, -limit, limit).astype(kind)


def setup_inputs(seed: int = 0) -> dict:
    key_list = jax.random.split(jax.random.key(seed), 7)
    return {
        "first_hidden_rows": draw_first_hidden_rows(jax.random.fold_in(key_list[6], 71), 0),
        "norm_scale": jnp.clip(1.0 + 0.18 * jax.random.normal(key_list[1], (MODEL_FEATURES,), jnp.float32), 0.1, 1.9),
        "projection_weight": noise(key_list[2], (MODEL_FEATURES, MODEL_FEATURES), MODEL_FEATURES ** -0.5, 0.109375, ((0, 8),)),
        "down_weights": noise(key_list[3], (ADAPTER_COUNT, MODEL_FEATURES, ADAPTER_RANK), MODEL_FEATURES ** -0.5, 0.109375, ((0, 64), (1, 8))),
        "up_weights": noise(key_list[4], (ADAPTER_COUNT, ADAPTER_RANK, MODEL_FEATURES), ADAPTER_RANK ** -0.5, 0.75, ((0, 64), (2, 8))),
        "requests": draw_requests(jax.random.fold_in(key_list[6], 71), 0),
    }


EPSILON = 1e-06

def reference(first_hidden_rows, norm_scale, projection_weight, down_weights, up_weights, requests):
    part_width = MODEL_FEATURES // N_TP

    def adapter_grouping(matmul_inputs):
        group_rows, adapter_index = matmul_inputs
        down_adapter = jnp.take(down_weights, adapter_index, axis=0).astype(jnp.float32)
        rank_rows = jnp.einsum('jbd,jdr->jbr', group_rows.astype(jnp.float32), down_adapter, precision=lax.Precision.HIGHEST).astype(jnp.bfloat16)
        up_adapter = jnp.take(up_weights, adapter_index, axis=0).astype(jnp.float32)
        return jnp.einsum('jbr,jrd->jbd', rank_rows.astype(jnp.float32), up_adapter, precision=lax.Precision.HIGHEST).astype(jnp.bfloat16)
    draft_states = first_hidden_rows
    outputs = []
    for draft_step in range(DRAFT):
        widened_output = draft_states.astype(jnp.float32)
        mean_square = lax.optimization_barrier(jnp.mean(widened_output * widened_output, axis=1, keepdims=True))
        normalized_rows = (widened_output * lax.rsqrt(mean_square + EPSILON) * norm_scale[None, :]).astype(jnp.bfloat16)
        base_output = jnp.zeros((TOTAL_ROWS, MODEL_FEATURES), jnp.float32)
        for shard in range(N_TP):
            lower = shard * part_width
            partial_value = jnp.dot(normalized_rows[:, lower:lower + part_width].astype(jnp.float32), projection_weight[lower:lower + part_width, :].astype(jnp.float32), precision=lax.Precision.HIGHEST)
            base_output = base_output + lax.optimization_barrier(partial_value.astype(jnp.bfloat16)).astype(jnp.float32)
        adapter_update = lax.map(adapter_grouping, (normalized_rows.reshape(N_REP, REQUEST_BLOCKS, BLOCK_LENGTH, MODEL_FEATURES), requests))
        draft_states = (widened_output + base_output + adapter_update.reshape(TOTAL_ROWS, MODEL_FEATURES).astype(jnp.float32)).astype(jnp.bfloat16)
        outputs.append(draft_states)
    return jnp.stack(outputs)
```

```python
import jax
import jax.numpy as jnp
from jax import lax
from jax.sharding import PartitionSpec as P

DRAFT = 2

EPSILON = 1e-06


def shards(first_hidden_rows, norm_scale, projection_weight, down_weights, up_weights, requests):
    groups = lax.axis_size("rep")
    tp = lax.axis_size("tp")
    rows, width = first_hidden_rows.shape
    full_width = width * tp
    kept, _, rank = down_weights.shape
    req_count = requests.shape[1]
    block_rows = rows // req_count
    bf16, f32 = jnp.bfloat16, jnp.float32

    me = lax.axis_index("rep")
    owners = requests // kept
    my_owner = jnp.take(owners, me, axis=0)
    to_holder = (my_owner[None, :] == jnp.arange(groups, dtype=jnp.int32)[:, None]).astype(bf16)
    held = jnp.sum(jnp.where(owners == me, requests % kept, 0), axis=1)
    row_adapter = jnp.repeat(held, block_rows)

    def move(blocks):
        return lax.all_to_all(blocks, "rep", split_axis=0, concat_axis=0, tiled=True)

    blocks = first_hidden_rows.reshape(req_count, block_rows * width)
    sent = jnp.dot(to_holder, blocks, preferred_element_type=f32).astype(bf16)
    states = move(sent).reshape(rows, width)
    down = jnp.transpose(down_weights, (1, 0, 2)).reshape(width, kept * rank)
    up = up_weights.reshape(kept * rank, width)
    mask = row_adapter[:, None] == jnp.arange(kept, dtype=jnp.int32)[None, :]
    outputs = []
    for step in range(DRAFT):
        wide = states.astype(f32)
        squares = jnp.sum(wide * wide, axis=1)
        scaled = (wide * norm_scale[None, :]).astype(bf16)
        partial = jnp.dot(scaled, projection_weight, preferred_element_type=f32).astype(bf16)
        ranks = jnp.dot(scaled, down, preferred_element_type=f32).reshape(rows, kept, rank)
        ranks = jnp.sum(jnp.where(mask[:, :, None], ranks, 0.0), axis=1).astype(bf16)
        high = squares.astype(bf16)
        low = (squares - high.astype(f32)).astype(bf16)
        extra = jnp.concatenate(
            [ranks, high[:, None], low[:, None], jnp.zeros((rows, 128 - rank - 2), bf16)], axis=1
        )
        sends = jnp.concatenate(
            [
                jnp.transpose(partial.reshape(rows, tp, width), (1, 0, 2)),
                jnp.broadcast_to(extra[None], (tp, rows, 128)),
            ],
            axis=2,
        )
        got = lax.all_to_all(sends, "tp", split_axis=0, concat_axis=0, tiled=True)
        total = jnp.sum(got.astype(f32), axis=0)
        mean = (total[:, width + rank] + total[:, width + rank + 1]) / full_width
        factor = lax.rsqrt(mean + EPSILON)[:, None]
        base = total[:, :width] * factor
        rank_rows = (total[:, width : width + rank] * factor).astype(bf16)
        spread = jnp.where(mask[:, :, None], rank_rows[:, None, :], 0).reshape(rows, kept * rank)
        delta = jnp.dot(spread, up, preferred_element_type=f32).astype(bf16)
        states = (wide + base + delta.astype(f32)).astype(bf16)
        home = move(states.reshape(req_count, block_rows * width))
        back = jnp.dot(to_holder.T, home, preferred_element_type=f32).astype(bf16)
        outputs.append(back.reshape(rows, width))
    return jnp.stack(outputs)


def solution(mesh):
    return jax.shard_map(
        shards,
        mesh=mesh,
        in_specs=(
            P("rep", "tp"),
            P("tp"),
            P("tp", None),
            P("rep", "tp", None),
            P("rep", None, "tp"),
            P(),
        ),
        out_specs=P(None, "rep", "tp"),
        check_vma=False,
    )
```

```python
import jax
import jax.numpy as jnp
from jax import lax
from jax.sharding import Mesh, PartitionSpec as P

DRAFT = 2

EPSILON = 1e-06


def pieces(values, count):
    found = []
    for _ in range(count):
        piece = lax.reduce_precision(values, 8, 7)
        found.append(piece.astype(jnp.bfloat16))
        values = values - piece
    return found


def shards(first_hidden_rows, norm_scale, projection_weight, down_weights, up_weights, requests):
    groups = lax.axis_size("rep")
    chips = lax.axis_size("y")
    cores = lax.axis_size("c")
    rows, width = first_hidden_rows.shape
    chip_width = width * cores
    full_width = chip_width * chips
    kept, _, rank = down_weights.shape
    req_count = requests.shape[1]
    block_rows = rows // req_count
    bf16, f32 = jnp.bfloat16, jnp.float32

    me = lax.axis_index("rep")
    core = lax.axis_index("c")
    owners = requests // kept
    my_owner = lax.dynamic_index_in_dim(owners, me, 0, keepdims=False)
    source_row = jnp.arange(rows, dtype=jnp.int32)
    target_row = jnp.repeat(my_owner * block_rows, block_rows) + source_row % block_rows
    to_holder = (target_row[None, :] == source_row[:, None]).astype(bf16)
    held = jnp.sum(jnp.where(owners == me, requests % kept, 0), axis=1)
    mask = held[:, None] == jnp.arange(kept, dtype=jnp.int32)[None, :]

    sent = jnp.dot(to_holder, first_hidden_rows, preferred_element_type=f32).astype(bf16)
    states = lax.all_to_all(
        sent.reshape(rows, 1, width), ("rep", "c"), split_axis=0, concat_axis=0, tiled=True
    ).reshape(groups, chip_width)

    sibling = [(i, cores - 1 - i) for i in range(cores)]
    down = jnp.transpose(down_weights, (0, 2, 1)).reshape(kept * rank, width)
    up = up_weights.reshape(kept * rank, width)
    gains = jnp.stack(pieces(norm_scale, 3) + [jnp.zeros((width,), bf16)] * 13)
    other_weight = lax.ppermute(projection_weight, "c", sibling)
    others = lax.ppermute(jnp.concatenate([down, up, gains]), "c", sibling)
    other_down, other_up = others[: kept * rank], others[kept * rank : 2 * kept * rank]
    other_scale = jnp.sum(others[2 * kept * rank :].astype(f32), axis=0)
    first = core == 0

    def halves(values):
        low, high = values[:, :width], values[:, width:]
        return jnp.where(first, low, high), jnp.where(first, high, low)

    def whole(mine, other):
        return jnp.concatenate(
            [jnp.where(first, mine, other), jnp.where(first, other, mine)], axis=1
        )

    scale = whole(norm_scale[None], other_scale[None])
    count = groups
    outputs = []
    for step in range(DRAFT):
        wide = states.astype(f32)
        squares = jnp.sum(wide * wide, axis=1)
        mine, other = halves((wide * scale).astype(bf16))
        partial = (
            jnp.dot(mine, projection_weight, preferred_element_type=f32)
            + jnp.dot(other, other_weight, preferred_element_type=f32)
        ).astype(bf16)
        contract = (((1,), (1,)), ((), ()))
        ranks = lax.dot_general(mine, down, contract, preferred_element_type=f32) + lax.dot_general(
            other, other_down, contract, preferred_element_type=f32
        )
        ranks = jnp.sum(
            jnp.where(mask[:, :, None], ranks.reshape(count, kept, rank), 0.0), axis=1
        ).astype(bf16)
        extra = jnp.concatenate(
            [ranks]
            + [piece[:, None] for piece in pieces(squares, 2)]
            + [jnp.zeros((count, 128 - rank - 2), bf16)],
            axis=1,
        )
        sends = jnp.concatenate(
            [
                jnp.transpose(partial.reshape(count, chips, chip_width), (1, 0, 2)),
                jnp.broadcast_to(extra[None], (chips, count, 128)),
            ],
            axis=2,
        )
        got = lax.all_to_all(sends, "y", split_axis=0, concat_axis=0, tiled=True)
        total = jnp.sum(got.astype(f32), axis=0)
        mean = (total[:, chip_width + rank] + total[:, chip_width + rank + 1]) / full_width
        factor = lax.rsqrt(mean + EPSILON)[:, None]
        rank_rows = (total[:, chip_width : chip_width + rank] * factor).astype(bf16)
        spread = jnp.where(mask[:, :, None], rank_rows[:, None, :], 0).reshape(count, kept * rank)
        delta = whole(
            jnp.dot(spread, up, preferred_element_type=f32),
            jnp.dot(spread, other_up, preferred_element_type=f32),
        ).astype(bf16)
        states = (wide + total[:, :chip_width] * factor + delta.astype(f32)).astype(bf16)
        outputs.append(states.reshape(count, cores, 1, width))
    back = jnp.concatenate(outputs, axis=2).reshape(count * cores, DRAFT, width)
    home = lax.all_to_all(back, ("rep", "c"), split_axis=0, concat_axis=0, tiled=True)
    from_holder = (target_row[:, None] == source_row[None, :]).astype(bf16)
    result = jnp.dot(
        from_holder, home.reshape(rows, DRAFT * width), preferred_element_type=f32
    ).astype(bf16)
    return jnp.transpose(result.reshape(rows, DRAFT, width), (1, 0, 2))


def solution(mesh):
    chip_mesh = Mesh(mesh.devices.reshape(mesh.shape["rep"], -1, 2), ("rep", "y", "c"))
    tp = ("y", "c")
    return jax.shard_map(
        shards,
        mesh=chip_mesh,
        in_specs=(
            P("rep", tp),
            P(tp),
            P(tp, None),
            P("rep", tp, None),
            P("rep", None, tp),
            P(),
        ),
        out_specs=P(None, "rep", tp),
        check_vma=False,
    )
```

```python
import functools

import jax
import jax.numpy as jnp
from jax import lax
from jax.experimental import pallas as pl
from jax.experimental.pallas import tpu as pltpu
from jax.sharding import Mesh, PartitionSpec as P

DRAFT = 2
LANES = 128
EPSILON = 1e-06

bf16, f32, i32 = jnp.bfloat16, jnp.float32, jnp.int32


def iota(shape, dim):
    return lax.broadcasted_iota(i32, shape, dim)


def mm(left, right):
    return jnp.dot(left, right, preferred_element_type=f32)


def mm_t(left, right):
    return lax.dot_general(left, right, (((1,), (1,)), ((), ())), preferred_element_type=f32)


def holder_rows(my_requests, kept, blocks):
    rows = 2 * blocks
    repeat = (iota((blocks, rows), 1) // 2 == iota((blocks, rows), 0)).astype(bf16)
    owner = jnp.broadcast_to((my_requests // kept).astype(f32).astype(bf16), (8, blocks))
    return mm(owner, repeat)[:1].astype(i32) * 2 + iota((1, rows), 1) % 2


def held_column(requests, me, kept):
    return jnp.sum(jnp.where(requests // kept == me, requests % kept, 0), axis=1, keepdims=True)


def permute_in(kept, requests_ref, x_ref, sent_ref):
    me = lax.axis_index("rep")
    blocks = requests_ref.shape[1]
    target = holder_rows(requests_ref[pl.ds(me, 1), :], kept, blocks)
    pick = (target == iota((2 * blocks, 2 * blocks), 0)).astype(bf16)
    sent_ref[...] = mm(pick, x_ref[...]).astype(bf16)


def permute_out(kept, requests_ref, home_ref, out_ref):
    me = lax.axis_index("rep")
    blocks = requests_ref.shape[1]
    width = out_ref.shape[2]
    target = holder_rows(requests_ref[pl.ds(me, 1), :], kept, blocks)
    pick = (target == iota((2 * blocks, 2 * blocks), 0)).astype(bf16)
    for step in range(DRAFT):
        out_ref[step] = lax.dot_general(
            pick,
            home_ref[:, step * width : (step + 1) * width],
            (((0,), (0,)), ((), ())),
            preferred_element_type=f32,
        ).astype(bf16)


def products(low, high, held, kept, weights, message_ref):
    weight, other_weight, down, other_down, scale, other_scale = weights
    first = lax.axis_index("c") == 0
    count, width = low.shape
    rank_cols = down.shape[0]
    rank = rank_cols // kept
    chips, _, packed = message_ref.shape
    chip_width = packed - LANES
    squares = jnp.sum(low * low, axis=1, keepdims=True) + jnp.sum(
        high * high, axis=1, keepdims=True
    )
    mine = (jnp.where(first, low, high) * scale[...]).astype(bf16)
    other = (jnp.where(first, high, low) * other_scale[...]).astype(bf16)
    for chip in range(chips):
        cols = pl.ds(chip * chip_width, chip_width)
        message_ref[chip, :, :chip_width] = (
            mm(mine, weight[:, cols]) + mm(other, other_weight[:, cols])
        ).astype(bf16)
    ranks = (mm_t(mine, down[...]) + mm_t(other, other_down[...])).astype(bf16)
    ranks = jnp.where(iota((count, rank_cols), 1) // rank == held, ranks, 0).astype(bf16)
    fold = iota((rank_cols, LANES), 0) % rank == iota((rank_cols, LANES), 1)
    extra = mm(ranks, fold.astype(bf16))
    top = squares.astype(bf16).astype(f32)
    lane = iota((count, LANES), 1)
    extra = jnp.where(lane == rank, top, extra)
    extra = jnp.where(lane == rank + 1, squares - top, extra).astype(bf16)
    for chip in range(chips):
        message_ref[chip, :, chip_width:] = extra


def update(low, high, held, kept, got_ref, up, other_up):
    first = lax.axis_index("c") == 0
    count, width = low.shape
    rank_cols = up.shape[0]
    rank = rank_cols // kept
    chips, _, packed = got_ref.shape
    chip_width = packed - LANES

    def total(start, stop):
        value = got_ref[0, :, start:stop].astype(f32)
        for chip in range(1, chips):
            value += got_ref[chip, :, start:stop].astype(f32)
        return value

    extra = total(chip_width, packed)
    lane = iota((count, LANES), 1)
    is_square = (lane == rank) | (lane == rank + 1)
    mean = jnp.sum(jnp.where(is_square, extra, 0.0), axis=1, keepdims=True) / (chip_width * chips)
    factor = lax.rsqrt(mean + EPSILON)
    ranks = jnp.where(lane < rank, extra * factor, 0.0).astype(bf16)
    unfold = iota((LANES, rank_cols), 1) % rank == iota((LANES, rank_cols), 0)
    spread = mm(ranks, unfold.astype(bf16))
    spread = jnp.where(iota((count, rank_cols), 1) // rank == held, spread, 0.0).astype(bf16)
    mine, other = mm(spread, up[...]), mm(spread, other_up[...])
    low_delta = jnp.where(first, mine, other).astype(bf16).astype(f32)
    high_delta = jnp.where(first, other, mine).astype(bf16).astype(f32)
    low = (low + total(0, width) * factor + low_delta).astype(bf16)
    high = (high + total(width, chip_width) * factor + high_delta).astype(bf16)
    return low, high


def row_pick(rows, core):
    return (iota((rows // 2, rows), 1) == 2 * iota((rows // 2, rows), 0) + core).astype(bf16)


def first_products(kept, requests_ref, x_ref, *refs):
    weights, message_ref = refs[:-1], refs[-1]
    held = held_column(requests_ref[...], lax.axis_index("rep"), kept)
    low, high = (mm(row_pick(x_ref.shape[0], core), x_ref[...]) for core in range(2))
    products(low, high, held, kept, weights, message_ref)


def next_products(kept, requests_ref, x_ref, got_ref, up, other_up, *refs):
    weights, (message_ref, state_ref) = refs[:-2], refs[-2:]
    held = held_column(requests_ref[...], lax.axis_index("rep"), kept)
    low, high = (mm(row_pick(x_ref.shape[0], core), x_ref[...]) for core in range(2))
    low, high = update(low, high, held, kept, got_ref, up, other_up)
    width = x_ref.shape[1]
    state_ref[:, :width] = low
    state_ref[:, width:] = high
    products(low.astype(f32), high.astype(f32), held, kept, weights, message_ref)


def last_update(kept, requests_ref, state_ref, got_ref, up, other_up, back_ref):
    held = held_column(requests_ref[...], lax.axis_index("rep"), kept)
    width = up.shape[1]
    rows = back_ref.shape[0]
    old = (state_ref[:, :width], state_ref[:, width:])
    new = update(old[0].astype(f32), old[1].astype(f32), held, kept, got_ref, up, other_up)
    for step, (low, high) in enumerate((old, new)):
        back_ref[:, step * width : (step + 1) * width] = sum(
            lax.dot_general(
                row_pick(rows, core), half, (((0,), (0,)), ((), ())), preferred_element_type=f32
            )
            for core, half in enumerate((low, high))
        ).astype(bf16)


def call(kernel, outs, *operands):
    spec = pl.BlockSpec(memory_space=pltpu.VMEM)
    return pl.pallas_call(
        kernel,
        out_shape=[jax.ShapeDtypeStruct(shape, bf16) for shape in outs],
        in_specs=[spec] * len(operands),
        out_specs=[spec] * len(outs),
        compiler_params=pltpu.CompilerParams(vmem_limit_bytes=24 * 2**20),
    )(*[pltpu.with_memory_space_constraint(operand, pltpu.VMEM) for operand in operands])


def shards(first_hidden_rows, norm_scale, projection_weight, down_weights, up_weights, requests):
    groups = lax.axis_size("rep")
    chips = lax.axis_size("y")
    cores = lax.axis_size("c")
    rows, width = first_hidden_rows.shape
    chip_width = width * cores
    kept, _, rank = down_weights.shape

    (sent,) = call(
        functools.partial(permute_in, kept), [(rows, width)], requests, first_hidden_rows
    )
    got = lax.all_to_all(
        sent.reshape(rows, 2, width // 2), ("rep", "c"), split_axis=0, concat_axis=0, tiled=True
    ).reshape(rows, width)

    sibling = [(i, cores - 1 - i) for i in range(cores)]
    down = jnp.transpose(down_weights, (0, 2, 1)).reshape(kept * rank, width)
    up = up_weights.reshape(kept * rank, width)
    scale = norm_scale[None]
    other_weight, other_down, other_up, other_scale = (
        lax.ppermute(value, "c", sibling) for value in (projection_weight, down, up, scale)
    )
    weights = (projection_weight, other_weight, down, other_down, scale, other_scale)

    def exchange(message):
        return lax.all_to_all(message, "y", split_axis=0, concat_axis=0, tiled=True)

    message_shape = (chips, groups, chip_width + LANES)
    (message,) = call(
        functools.partial(first_products, kept), [message_shape], requests, got, *weights
    )
    message, state = call(
        functools.partial(next_products, kept),
        [message_shape, (groups, chip_width)],
        requests,
        got,
        exchange(message),
        up,
        other_up,
        *weights,
    )
    (back,) = call(
        functools.partial(last_update, kept),
        [(rows, DRAFT * width)],
        requests,
        state,
        exchange(message),
        up,
        other_up,
    )
    home = lax.all_to_all(
        back.reshape(rows, DRAFT, width), ("rep", "c"), split_axis=0, concat_axis=0, tiled=True
    ).reshape(rows, DRAFT * width)
    (result,) = call(
        functools.partial(permute_out, kept), [(DRAFT, rows, width)], requests, home
    )
    return result


def solution(mesh):
    chip_mesh = Mesh(mesh.devices.reshape(mesh.shape["rep"], -1, 2), ("rep", "y", "c"))
    tp = ("y", "c")
    return jax.shard_map(
        shards,
        mesh=chip_mesh,
        in_specs=(
            P("rep", tp),
            P(tp),
            P(tp, None),
            P("rep", tp, None),
            P("rep", None, tp),
            P(),
        ),
        out_specs=P(None, "rep", tp),
        check_vma=False,
    )
```

```python
import functools

import jax
import jax.numpy as jnp
from jax import lax
from jax.experimental import pallas as pl
from jax.experimental.pallas import tpu as pltpu
from jax.sharding import Mesh, PartitionSpec as P

DRAFT = 2
LANES = 128
EPSILON = 1e-06
TURN = 34
TURN_Y = 2
SLOT = 4

bf16, f32, i32 = jnp.bfloat16, jnp.float32, jnp.int32


def iota(shape, dim):
    return lax.broadcasted_iota(i32, shape, dim)


def mm(left, right):
    return jnp.dot(left, right, preferred_element_type=f32)


def mm_t(left, right):
    return lax.dot_general(left, right, (((1,), (1,)), ((), ())), preferred_element_type=f32)


def t_mm(left, right):
    return lax.dot_general(left, right, (((0,), (0,)), ((), ())), preferred_element_type=f32)


def moved_rows(my_requests, kept, blocks):
    rows = 2 * blocks
    repeat = (iota((blocks, rows), 1) // 2 == iota((blocks, rows), 0)).astype(bf16)
    owner = jnp.broadcast_to((my_requests // kept).astype(f32).astype(bf16), (8, blocks))
    place = (mm(owner, repeat)[:1].astype(i32) + (blocks - TURN)) % blocks
    return place * 2 + iota((1, rows), 1) % 2


def permute_in(kept, requests_hbm, x_hbm, sent_ref, requests_ref, x_ref, sems):
    x_copy = pltpu.make_async_copy(x_hbm, x_ref, sems.at[0])
    requests_copy = pltpu.make_async_copy(requests_hbm, requests_ref, sems.at[1])
    x_copy.start()
    requests_copy.start()
    requests_copy.wait()
    me = lax.axis_index("rep")
    blocks = requests_ref.shape[1]
    rows = 2 * blocks
    target = SLOT * moved_rows(requests_ref[pl.ds(me, 1), :], kept, blocks)
    picks = [
        (target + part == iota((SLOT * rows, rows), 0)).astype(bf16)
        for part in range(x_ref.shape[1] // LANES)
    ]
    x_copy.wait()
    sent_ref[...] = sum(
        mm(pick, x_ref[:, part * LANES : (part + 1) * LANES]) for part, pick in enumerate(picks)
    ).astype(bf16)


def permute_out(kept, requests_ref, home_ref, out_ref):
    me = lax.axis_index("rep")
    blocks = requests_ref.shape[1]
    width = out_ref.shape[2]
    target = moved_rows(requests_ref[pl.ds(me, 1), :], kept, blocks)
    pick = (target == iota((2 * blocks, 2 * blocks), 0)).astype(bf16)
    for step in range(DRAFT):
        out_ref[step] = t_mm(pick, home_ref[:, step * width : (step + 1) * width]).astype(bf16)


def find_held(kept, requests_ref, held_ref):
    requests = requests_ref[...]
    groups = requests.shape[0]
    held = jnp.sum(
        jnp.where(requests // kept == lax.axis_index("rep"), requests % kept, 0),
        axis=1,
        keepdims=True,
    )
    held = jnp.broadcast_to(held.astype(f32), (groups, LANES)).astype(bf16)
    turn = (iota((groups, groups), 0) + TURN) % groups == iota((groups, groups), 1)
    held_ref[...] = mm(turn.astype(bf16), held).astype(i32)


def products(wide, kept, held_ref, weight, down, scale, message_ref, arrived=None):
    count, chip_width = wide.shape
    rank_cols = down.shape[0]
    rank = rank_cols // kept
    chips = message_ref.shape[0]
    scaled = (wide * scale[...]).astype(bf16)
    squares = jnp.sum(wide * wide, axis=1, keepdims=True)
    top = squares.astype(bf16).astype(f32)
    lane = iota((count, LANES), 1)
    fold = iota((rank_cols, LANES), 0) % rank == iota((rank_cols, LANES), 1)
    owned = iota((count, rank_cols), 1) // rank == held_ref[:, :1]
    if arrived is not None:
        arrived(0)
    ranks = mm_t(scaled, down[...]).astype(bf16)
    ranks = jnp.where(owned, ranks, 0).astype(bf16)
    extra = mm(ranks, fold.astype(bf16))
    extra = jnp.where(lane == rank, top, extra)
    extra = jnp.where(lane == rank + 1, squares - top, extra).astype(bf16)
    for place in range(chips):
        chip = (place + TURN_Y) % chips
        if arrived is not None:
            arrived(1 + chip)
        message_ref[place, :, :chip_width] = mm(
            scaled, weight[:, chip * chip_width : (chip + 1) * chip_width]
        ).astype(bf16)
        message_ref[place, :, chip_width:] = extra


def update(wide, kept, held_ref, got_ref, up):
    count, chip_width = wide.shape
    rank_cols = up.shape[0]
    rank = rank_cols // kept
    chips = got_ref.shape[0]
    total = got_ref[0].astype(f32)
    for chip in range(1, chips):
        total += got_ref[chip].astype(f32)
    extra = total[:, chip_width:]
    lane = iota((count, LANES), 1)
    is_square = (lane == rank) | (lane == rank + 1)
    mean = jnp.sum(jnp.where(is_square, extra, 0.0), axis=1, keepdims=True) / (chip_width * chips)
    factor = lax.rsqrt(mean + EPSILON)
    ranks = jnp.where(lane < rank, extra * factor, 0.0).astype(bf16)
    unfold = iota((LANES, rank_cols), 1) % rank == iota((LANES, rank_cols), 0)
    spread = mm(ranks, unfold.astype(bf16))
    owned = iota((count, rank_cols), 1) // rank == held_ref[:, :1]
    spread = jnp.where(owned, spread, 0.0).astype(bf16)
    delta = mm(spread, up[...]).astype(bf16).astype(f32)
    return (wide + total[:, :chip_width] * factor + delta).astype(bf16)


def moved_in(x_ref):
    slots, lanes = x_ref.shape
    groups = slots // (2 * SLOT)
    parts = [(core, part) for core in range(2) for part in range(SLOT - 1)]
    row, slot = iota((groups, slots), 0), iota((groups, slots), 1)
    picks = [(slot == (2 * row + core) * SLOT + part).astype(bf16) for core, part in parts]
    rows = mm(jnp.concatenate(picks), x_ref[...])
    return jnp.concatenate(
        [rows[index * groups : (index + 1) * groups] for index in range(len(parts))], axis=1
    )


def first_products(kept, *refs):
    matrices, (scale, other_scale, x_ref, held_ref) = refs[:6], refs[6:10]
    message_ref, wide_ref, weight_out, down_out, up_out, scale_out, sems = refs[10:]
    width = scale.shape[1]
    chip_width = 2 * width
    chips = message_ref.shape[0]
    core = lax.axis_index("c")
    pieces = [[] for _ in range(chips + 2)]

    def add(piece, source, target):
        index = sum(map(len, pieces))
        copy = pltpu.make_async_copy(source, target, sems.at[index])
        copy.start()
        pieces[piece].append(copy)

    places = [
        pl.ds(pl.multiple_of(jnp.where(core == index, 0, width), LANES), width)
        for index in range(2)
    ]
    for index in range(2):
        add(0, matrices[1 + 3 * index], down_out.at[:, places[index]])
    for place in range(chips):
        chip = (place + TURN_Y) % chips
        cols = pl.ds(chip * chip_width, chip_width)
        for index in range(2):
            add(1 + chip, matrices[3 * index].at[:, cols], weight_out.at[places[index], cols])
    for index in range(2):
        add(chips + 1, matrices[2 + 3 * index], up_out.at[:, places[index]])

    def arrived(piece):
        for copy in pieces[piece]:
            copy.wait()

    low = jnp.where(core == 0, scale[...], other_scale[...])
    high = jnp.where(core == 0, other_scale[...], scale[...])
    scale_out[...] = jnp.concatenate([low, high], axis=1)
    wide = moved_in(x_ref)
    wide_ref[...] = wide.astype(bf16)
    products(wide, kept, held_ref, weight_out, down_out, scale_out, message_ref, arrived)
    arrived(chips + 1)


def next_products(kept, wide_ref, got_ref, held_ref, weight, down, up, scale, message_ref, state_ref):
    state = update(wide_ref[...].astype(f32), kept, held_ref, got_ref, up)
    state_ref[...] = state
    products(state.astype(f32), kept, held_ref, weight, down, scale, message_ref)


def last_update(kept, state_ref, got_ref, held_ref, up, back_ref):
    rows, cols = back_ref.shape
    width = cols // DRAFT
    old = state_ref[...]
    new = update(old.astype(f32), kept, held_ref, got_ref, up)
    row, place = iota((rows // 2, rows), 0), iota((rows // 2, rows), 1)
    picks = [(place == 2 * row + core).astype(bf16) for core in range(2)]
    for step, state in enumerate((old, new)):
        back_ref[:, step * width : (step + 1) * width] = sum(
            t_mm(pick, state[:, core * width : (core + 1) * width])
            for core, pick in enumerate(picks)
        ).astype(bf16)


def call(kernel, outs, operands, far=0, loose=0, **kwargs):
    spaces = [pltpu.HBM] * far + [pl.ANY] * loose
    spaces += [pltpu.VMEM] * (len(operands) - len(spaces))
    return pl.pallas_call(
        kernel,
        out_shape=outs,
        in_specs=[pl.BlockSpec(memory_space=space) for space in spaces],
        out_specs=[pl.BlockSpec(memory_space=pltpu.VMEM)] * len(outs),
        compiler_params=pltpu.CompilerParams(vmem_limit_bytes=24 * 2**20),
        **kwargs,
    )(*map(pltpu.with_memory_space_constraint, operands, spaces))


def shards(first_hidden_rows, norm_scale, projection_weight, down_weights, up_weights, requests):
    groups = lax.axis_size("rep")
    chips = lax.axis_size("y")
    cores = lax.axis_size("c")
    rows, width = first_hidden_rows.shape
    chip_width = width * cores
    kept, _, rank = down_weights.shape
    rank_cols = kept * rank

    def resident(shape, dtype=bf16):
        return pltpu.VMEM(shape, dtype)

    (sent,) = call(
        functools.partial(permute_in, kept),
        [resident((SLOT * rows, LANES))],
        [requests, first_hidden_rows],
        far=2,
        scratch_shapes=[
            pltpu.VMEM(requests.shape, i32),
            pltpu.VMEM((rows, width), bf16),
            pltpu.SemaphoreType.DMA((2,)),
        ],
    )
    movers = [[(place + TURN * cores) % rows for place in range(rows)]]
    adders = [[(place + TURN_Y) % chips for place in range(chips)]]

    def move(value):
        return lax.all_to_all(
            value, ("rep", "c"), split_axis=0, concat_axis=0, axis_index_groups=movers, tiled=True
        )

    def exchange(message):
        return lax.all_to_all(
            message, "y", split_axis=0, concat_axis=0, axis_index_groups=adders, tiled=True
        )

    got = move(sent.reshape(rows, SLOT, LANES)).reshape(SLOT * rows, LANES)

    sibling = [(core, cores - 1 - core) for core in range(cores)]
    down = jnp.transpose(down_weights, (0, 2, 1)).reshape(rank_cols, width)
    up = up_weights.reshape(rank_cols, width)
    matrices = [projection_weight, down, up]
    others = [lax.ppermute(value, "c", sibling) for value in matrices]
    scale = norm_scale[None]
    (held,) = call(
        functools.partial(find_held, kept),
        [resident((groups, LANES), i32)],
        [requests],
    )

    message_shape = resident((chips, groups, chip_width + LANES))
    state_shape = resident((groups, chip_width))
    message, wide, weight, down, up, scale = call(
        functools.partial(first_products, kept),
        [
            message_shape,
            state_shape,
            resident((chip_width, projection_weight.shape[1])),
            resident((rank_cols, chip_width)),
            resident((rank_cols, chip_width)),
            resident((1, chip_width), f32),
        ],
        matrices + others + [scale, lax.ppermute(scale, "c", sibling), got, held],
        far=len(matrices),
        loose=len(others),
        scratch_shapes=[pltpu.SemaphoreType.DMA((2 * chips + 4,))],
    )
    message, state = call(
        functools.partial(next_products, kept),
        [message_shape, state_shape],
        [wide, exchange(message), held, weight, down, up, scale],
    )
    (back,) = call(
        functools.partial(last_update, kept),
        [resident((rows, DRAFT * width))],
        [state, exchange(message), held, up],
    )
    home = move(back.reshape(rows, DRAFT, width)).reshape(rows, DRAFT * width)
    (result,) = call(
        functools.partial(permute_out, kept),
        [jax.ShapeDtypeStruct((DRAFT, rows, width), bf16)],
        [requests, home],
    )
    return result


def solution(mesh):
    chip_mesh = Mesh(mesh.devices.reshape(mesh.shape["rep"], -1, 2), ("rep", "y", "c"))
    tp = ("y", "c")
    return jax.shard_map(
        shards,
        mesh=chip_mesh,
        in_specs=(
            P("rep", tp),
            P(tp),
            P(tp, None),
            P("rep", tp, None),
            P("rep", None, tp),
            P(),
        ),
        out_specs=P(None, "rep", tp),
        check_vma=False,
    )
```

```python
import functools

import jax
import jax.numpy as jnp
from jax import lax
from jax.experimental import pallas as pl
from jax.experimental.pallas import tpu as pltpu
from jax.sharding import Mesh, PartitionSpec as P

DRAFT = 2
LANES = 128
EPSILON = 1e-06
TURN = 34
TURN_Y = 2
HINT = 2 * 10**11
SLOT = 4

bf16, f32, i32 = jnp.bfloat16, jnp.float32, jnp.int32


def iota(shape, dim):
    return lax.broadcasted_iota(i32, shape, dim)


def mm(left, right):
    return jnp.dot(left, right, preferred_element_type=f32)


def mm_t(left, right):
    return lax.dot_general(left, right, (((1,), (1,)), ((), ())), preferred_element_type=f32)


def t_mm(left, right):
    return lax.dot_general(left, right, (((0,), (0,)), ((), ())), preferred_element_type=f32)


def holder_places(my_requests, kept):
    blocks = my_requests.shape[1]
    return (my_requests // kept + (blocks - TURN)) % blocks


def split(values):
    high = values.astype(bf16).astype(f32)
    middle = (values - high).astype(bf16).astype(f32)
    return high, middle, values - high - middle


def permute_in(kept, requests_hbm, x_hbm, scale_hbm, sent_ref, requests_ref, x_ref, scale_ref, sems):
    copies = [
        pltpu.make_async_copy(source, target, sems.at[index])
        for index, (source, target) in enumerate(
            ((requests_hbm, requests_ref), (x_hbm, x_ref), (scale_hbm, scale_ref))
        )
    ]
    for copy in copies:
        copy.start()
    me = lax.axis_index("rep")
    blocks = requests_ref.shape[1]
    rows, width = x_ref.shape
    slots = sent_ref.shape[0]
    parts = width // LANES
    row_picks = [
        (iota((blocks, rows), 1) == 2 * iota((blocks, rows), 0) + half).astype(bf16)
        for half in range(2)
    ]
    piece, block = iota((slots, 2 * parts * blocks), 1) // blocks, iota((slots, 2 * parts * blocks), 1) % blocks
    slot = (2 * block + piece // parts) * SLOT + piece % parts
    lay_out = (iota((slots, 2 * parts * blocks), 0) == slot).astype(bf16)
    copies[1].wait()
    halves = [mm(pick, x_ref[...]).astype(bf16) for pick in row_picks]
    copies[2].wait()
    wanted = (me + (blocks - TURN)) % blocks % (3 * parts)
    gain = jnp.zeros((1, LANES), f32)
    for part in range(parts):
        for index, value in enumerate(split(scale_ref[part : part + 1, :])):
            gain = jnp.where(wanted == 3 * part + index, value, gain)
    copies[0].wait()
    places = holder_places(requests_ref[pl.ds(me, 1), :], kept)
    pick = (places == iota((blocks, blocks), 0)).astype(bf16)
    picked = [mm(pick, half).astype(bf16) for half in halves]
    stacked = jnp.concatenate(
        [half[:, part * LANES : (part + 1) * LANES] for half in picked for part in range(parts)]
    )
    padding = iota((slots, LANES), 0) % SLOT == parts
    sent_ref[...] = jnp.where(padding, gain, mm(lay_out, stacked)).astype(bf16)


def permute_out(kept, requests_ref, home_ref, out_ref):
    me = lax.axis_index("rep")
    blocks = requests_ref.shape[1]
    rows, width = out_ref.shape[1:]
    repeat = (iota((blocks, rows), 1) // 2 == iota((blocks, rows), 0)).astype(bf16)
    places = holder_places(requests_ref[pl.ds(me, 1), :], kept)
    places = jnp.broadcast_to(places.astype(f32), (8, blocks)).astype(bf16)
    target = mm(places, repeat)[:1].astype(i32) * 2 + iota((1, rows), 1) % 2
    pick = (target == iota((rows, rows), 0)).astype(bf16)
    for step in range(DRAFT):
        out_ref[step] = t_mm(pick, home_ref[:, step * width : (step + 1) * width]).astype(bf16)


def find_held(kept, requests_hbm, held_ref, requests_ref, sem):
    copy = pltpu.make_async_copy(requests_hbm, requests_ref, sem)
    copy.start()
    copy.wait()
    requests = requests_ref[...]
    groups = requests.shape[0]
    held = jnp.sum(
        jnp.where(requests // kept == lax.axis_index("rep"), requests % kept, 0),
        axis=1,
        keepdims=True,
    )
    held = jnp.broadcast_to(held.astype(f32), (groups, LANES)).astype(bf16)
    turn = (iota((groups, groups), 0) + TURN) % groups == iota((groups, groups), 1)
    held_ref[...] = mm(turn.astype(bf16), held).astype(i32)


def products(wide, kept, held_ref, weight, down, scale, message_ref, arrived=None):
    count, chip_width = wide.shape
    rank_cols = down.shape[0]
    rank = rank_cols // kept
    chips = message_ref.shape[0]
    scaled = (wide * scale[...]).astype(bf16)
    squares = jnp.sum(wide * wide, axis=1, keepdims=True)
    top = squares.astype(bf16).astype(f32)
    lane = iota((count, LANES), 1)
    fold = iota((rank_cols, LANES), 0) % rank == iota((rank_cols, LANES), 1)
    owned = iota((count, rank_cols), 1) // rank == held_ref[:, :1]
    if arrived is not None:
        arrived(0)
    ranks = mm_t(scaled, down[...]).astype(bf16)
    ranks = jnp.where(owned, ranks, 0).astype(bf16)
    extra = mm(ranks, fold.astype(bf16))
    extra = jnp.where(lane == rank, top, extra)
    extra = jnp.where(lane == rank + 1, squares - top, extra).astype(bf16)
    for place in range(chips):
        chip = (place + TURN_Y) % chips
        if arrived is not None:
            arrived(1 + chip)
        message_ref[place, :, :chip_width] = mm(
            scaled, weight[:, chip * chip_width : (chip + 1) * chip_width]
        ).astype(bf16)
        message_ref[place, :, chip_width:] = extra


def update(wide, kept, held_ref, got_ref, up):
    count, chip_width = wide.shape
    rank_cols = up.shape[0]
    rank = rank_cols // kept
    chips = got_ref.shape[0]
    total = got_ref[0].astype(f32)
    for chip in range(1, chips):
        total += got_ref[chip].astype(f32)
    extra = total[:, chip_width:]
    lane = iota((count, LANES), 1)
    is_square = (lane == rank) | (lane == rank + 1)
    mean = jnp.sum(jnp.where(is_square, extra, 0.0), axis=1, keepdims=True) / (chip_width * chips)
    factor = lax.rsqrt(mean + EPSILON)
    ranks = jnp.where(lane < rank, extra * factor, 0.0).astype(bf16)
    unfold = iota((LANES, rank_cols), 1) % rank == iota((LANES, rank_cols), 0)
    spread = mm(ranks, unfold.astype(bf16))
    owned = iota((count, rank_cols), 1) // rank == held_ref[:, :1]
    spread = jnp.where(owned, spread, 0.0).astype(bf16)
    delta = mm(spread, up[...]).astype(bf16).astype(f32)
    return (wide + total[:, :chip_width] * factor + delta).astype(bf16)


def moved_in(x_ref):
    slots, lanes = x_ref.shape
    groups = slots // (2 * SLOT)
    parts = [(core, part) for core in range(2) for part in range(SLOT - 1)]
    row, slot = iota((groups, slots), 0), iota((groups, slots), 1)
    picks = [(slot == (2 * row + core) * SLOT + part).astype(bf16) for core, part in parts]
    row, slot = iota((16, slots), 0), iota((16, slots), 1)
    place, core = slot // (2 * SLOT), slot // SLOT % 2
    padding = (slot % SLOT == SLOT - 1) & (place < 3 * (SLOT - 1))
    picks.append((padding & (row == core * (SLOT - 1) + place // 3)).astype(bf16))
    rows = mm(jnp.concatenate(picks), x_ref[...])
    gains = rows[len(parts) * groups :]
    wide = jnp.concatenate(
        [rows[index * groups : (index + 1) * groups] for index in range(len(parts))], axis=1
    )
    return wide, jnp.concatenate([gains[index : index + 1] for index in range(len(parts))], axis=1)


def first_products(kept, *refs):
    (x_ref, held_ref), matrices = refs[:2], (refs[5:8], refs[2:5])
    message_ref, wide_ref, weight_out, down_out, up_out, scale_out, sems = refs[8:]
    chip_width = wide_ref.shape[1]
    width = chip_width // 2
    chips = message_ref.shape[0]
    core = lax.axis_index("c")
    pieces = [[] for _ in range(chips + 2)]

    def add(piece, source, target):
        index = sum(map(len, pieces))
        copy = pltpu.make_async_copy(source, target, sems.at[index])
        copy.start()
        pieces[piece].append(copy)

    places = [
        pl.ds(pl.multiple_of(jnp.where(core == index, 0, width), LANES), width)
        for index in range(2)
    ]
    for index in range(2):
        add(0, matrices[index][0], down_out.at[:, places[index]])
    for place in range(chips):
        chip = (place + TURN_Y) % chips
        cols = pl.ds(chip * chip_width, chip_width)
        for index in range(2):
            add(1 + chip, matrices[index][2].at[:, cols], weight_out.at[places[index], cols])
    for index in range(2):
        add(chips + 1, matrices[index][1], up_out.at[:, places[index]])

    def arrived(piece):
        for copy in pieces[piece]:
            copy.wait()

    wide, scale = moved_in(x_ref)
    scale_out[...] = scale
    wide_ref[...] = wide.astype(bf16)
    products(wide, kept, held_ref, weight_out, down_out, scale_out, message_ref, arrived)
    arrived(chips + 1)


def next_products(kept, wide_ref, got_ref, held_ref, weight, down, up, scale, message_ref, state_ref):
    state = update(wide_ref[...].astype(f32), kept, held_ref, got_ref, up)
    state_ref[...] = state
    products(state.astype(f32), kept, held_ref, weight, down, scale, message_ref)


def last_update(kept, state_ref, got_ref, held_ref, up, back_ref):
    rows, cols = back_ref.shape
    width = cols // DRAFT
    old = state_ref[...]
    new = update(old.astype(f32), kept, held_ref, got_ref, up)
    row, place = iota((rows // 2, rows), 0), iota((rows // 2, rows), 1)
    picks = [(place == 2 * row + core).astype(bf16) for core in range(2)]
    for step, state in enumerate((old, new)):
        back_ref[:, step * width : (step + 1) * width] = sum(
            t_mm(pick, state[:, core * width : (core + 1) * width])
            for core, pick in enumerate(picks)
        ).astype(bf16)


def call(kernel, outs, operands, far=0, **kwargs):
    spaces = [pltpu.VMEM] * (len(operands) - far) + [pltpu.HBM] * far
    return pl.pallas_call(
        kernel,
        out_shape=outs,
        in_specs=[pl.BlockSpec(memory_space=space) for space in spaces],
        out_specs=[pl.BlockSpec(memory_space=pltpu.VMEM)] * len(outs),
        compiler_params=pltpu.CompilerParams(vmem_limit_bytes=24 * 2**20),
        **kwargs,
    )(*map(pltpu.with_memory_space_constraint, operands, spaces))


def shards(first_hidden_rows, norm_scale, projection_weight, down_weights, up_weights, requests):
    groups = lax.axis_size("rep")
    chips = lax.axis_size("y")
    cores = lax.axis_size("c")
    rows, width = first_hidden_rows.shape
    chip_width = width * cores
    kept, _, rank = down_weights.shape
    rank_cols = kept * rank

    def resident(shape, dtype=bf16):
        return pltpu.VMEM(shape, dtype)

    (sent,) = call(
        functools.partial(permute_in, kept),
        [resident((SLOT * rows, LANES))],
        [requests, first_hidden_rows, norm_scale.reshape(-1, LANES)],
        far=3,
        scratch_shapes=[
            pltpu.VMEM(requests.shape, i32),
            pltpu.VMEM((rows, width), bf16),
            pltpu.VMEM((width // LANES, LANES), f32),
            pltpu.SemaphoreType.DMA((3,)),
        ],
    )
    movers = [[(place + TURN * cores) % rows for place in range(rows)]]
    adders = [[(place + TURN_Y) % chips for place in range(chips)]]

    def move(value):
        return lax.all_to_all(
            value, ("rep", "c"), split_axis=0, concat_axis=0, axis_index_groups=movers, tiled=True
        )

    def exchange(message):
        return lax.all_to_all(
            message, "y", split_axis=0, concat_axis=0, axis_index_groups=adders, tiled=True
        )

    got = move(sent.reshape(rows, SLOT, LANES)).reshape(SLOT * rows, LANES)

    sibling = [(core, cores - 1 - core) for core in range(cores)]
    down = jnp.transpose(down_weights, (0, 2, 1)).reshape(rank_cols, width)
    up = up_weights.reshape(rank_cols, width)
    matrices = [down, up, projection_weight]
    others = [lax.ppermute(value, "c", sibling) for value in matrices]
    (held,) = call(
        functools.partial(find_held, kept),
        [resident((groups, LANES), i32)],
        [requests],
        far=1,
        scratch_shapes=[pltpu.VMEM(requests.shape, i32), pltpu.SemaphoreType.DMA(())],
        cost_estimate=pl.CostEstimate(flops=HINT, bytes_accessed=0, transcendentals=0),
    )

    message_shape = resident((chips, groups, chip_width + LANES))
    state_shape = resident((groups, chip_width))
    message, wide, weight, down, up, scale = call(
        functools.partial(first_products, kept),
        [
            message_shape,
            state_shape,
            resident((chip_width, projection_weight.shape[1])),
            resident((rank_cols, chip_width)),
            resident((rank_cols, chip_width)),
            resident((1, chip_width), f32),
        ],
        [got, held] + others + matrices,
        far=len(matrices),
        scratch_shapes=[pltpu.SemaphoreType.DMA((2 * chips + 4,))],
    )
    message, state = call(
        functools.partial(next_products, kept),
        [message_shape, state_shape],
        [wide, exchange(message), held, weight, down, up, scale],
    )
    (back,) = call(
        functools.partial(last_update, kept),
        [resident((rows, DRAFT * width))],
        [state, exchange(message), held, up],
    )
    home = move(back.reshape(rows, DRAFT, width)).reshape(rows, DRAFT * width)
    (result,) = call(
        functools.partial(permute_out, kept),
        [jax.ShapeDtypeStruct((DRAFT, rows, width), bf16)],
        [requests, home],
    )
    return result


def solution(mesh):
    chip_mesh = Mesh(mesh.devices.reshape(mesh.shape["rep"], -1, 2), ("rep", "y", "c"))
    tp = ("y", "c")
    return jax.shard_map(
        shards,
        mesh=chip_mesh,
        in_specs=(
            P("rep", tp),
            P(tp),
            P(tp, None),
            P("rep", tp, None),
            P("rep", None, tp),
            P(),
        ),
        out_specs=P(None, "rep", tp),
        check_vma=False,
    )
```

```python
import functools

import jax
import jax.numpy as jnp
from jax import lax
from jax.experimental import pallas as pl
from jax.experimental.pallas import tpu as pltpu
from jax.sharding import Mesh, PartitionSpec as P

DRAFT = 2
LANES = 128
EPSILON = 1e-06
TURN = 34
TURN_Y = 2
HINT = 2 * 10**11
SLOT = 4

bf16, f32, i32 = jnp.bfloat16, jnp.float32, jnp.int32


def iota(shape, dim):
    return lax.broadcasted_iota(i32, shape, dim)


def over(values, size):
    return values >> (size.bit_length() - 1)


def within(values, size):
    return values & (size - 1)


def mm(left, right):
    return jnp.dot(left, right, preferred_element_type=f32)


def mm_t(left, right):
    return lax.dot_general(left, right, (((1,), (1,)), ((), ())), preferred_element_type=f32)


def t_mm(left, right):
    return lax.dot_general(left, right, (((0,), (0,)), ((), ())), preferred_element_type=f32)


def holder_places(my_requests, kept):
    blocks = my_requests.shape[1]
    return within(over(my_requests, kept) + (blocks - TURN), blocks)


def split(values):
    high = values.astype(bf16).astype(f32)
    middle = (values - high).astype(bf16).astype(f32)
    return high, middle, values - high - middle


def permute_in(kept, requests_hbm, x_hbm, scale_hbm, down_hbm, up_hbm, *refs):
    sent_ref, adapters_hbm, requests_ref, x_ref, scale_ref, sems = refs
    rank_cols = down_hbm.shape[0]
    copies = [
        pltpu.make_async_copy(source, target, sems.at[index])
        for index, (source, target) in enumerate(
            (
                (x_hbm, x_ref),
                (requests_hbm, requests_ref),
                (scale_hbm, scale_ref),
                (down_hbm, adapters_hbm.at[:rank_cols]),
                (up_hbm, adapters_hbm.at[rank_cols:]),
            )
        )
    ]
    for copy in copies:
        copy.start()
    me = lax.axis_index("rep")
    blocks = requests_ref.shape[1]
    rows, width = x_ref.shape
    slots = sent_ref.shape[0]
    parts = width // LANES
    row_picks = [
        (iota((blocks, rows), 1) == 2 * iota((blocks, rows), 0) + half).astype(bf16)
        for half in range(2)
    ]
    index = iota((1, 2 * parts * blocks), 1)
    piece, block = over(index, blocks), within(index, blocks)
    slot = 2 * SLOT * block + jnp.where(piece < parts, piece, SLOT + piece - parts)
    lay_out = (iota((slots, 2 * parts * blocks), 0) == slot).astype(bf16)
    padding = within(iota((slots, 1), 0), SLOT) == parts
    copies[0].wait()
    halves = [mm(pick, x_ref[...]).astype(bf16) for pick in row_picks]
    copies[1].wait()
    places = holder_places(requests_ref[pl.ds(me, 1), :], kept)
    pick = (places == iota((blocks, blocks), 0)).astype(bf16)
    picked = [mm(pick, half).astype(bf16) for half in halves]
    stacked = jnp.concatenate(
        [half[:, part * LANES : (part + 1) * LANES] for half in picked for part in range(parts)]
    )
    copies[2].wait()
    wanted = lax.rem(within(me + (blocks - TURN), blocks), 3 * parts)
    gain = jnp.zeros((1, LANES), f32)
    for part in range(parts):
        for number, value in enumerate(split(scale_ref[part : part + 1, :])):
            gain = jnp.where(wanted == 3 * part + number, value, gain)
    sent_ref[...] = jnp.where(padding, gain, mm(lay_out, stacked)).astype(bf16)
    for copy in copies[3:]:
        copy.wait()


def permute_out(kept, requests_ref, home_ref, out_ref):
    me = lax.axis_index("rep")
    blocks = requests_ref.shape[1]
    rows, width = out_ref.shape[1:]
    repeat = (over(iota((blocks, rows), 1), 2) == iota((blocks, rows), 0)).astype(bf16)
    places = holder_places(requests_ref[pl.ds(me, 1), :], kept)
    places = jnp.broadcast_to(places.astype(f32), (8, blocks)).astype(bf16)
    target = mm(places, repeat)[:1].astype(i32) * 2 + within(iota((1, rows), 1), 2)
    pick = (target == iota((rows, rows), 0)).astype(bf16)
    for step in range(DRAFT):
        out_ref[step] = t_mm(pick, home_ref[:, step * width : (step + 1) * width]).astype(bf16)


def unpack_picks(pick_ref):
    slots = pick_ref.shape[1]
    groups = over(slots, 2 * SLOT)
    parts = SLOT - 1
    row, slot = iota((groups, slots), 0), iota((groups, slots), 1)
    for core in range(2):
        for part in range(parts):
            start = (core * parts + part) * groups
            hit = slot == (2 * row + core) * SLOT + part
            pick_ref[start : start + groups, :] = hit.astype(bf16)
    row, slot = iota((16, slots), 0), iota((1, slots), 1)
    place, core = over(slot, 2 * SLOT), within(over(slot, SLOT), 2)
    part = (place >= 3).astype(i32) + (place >= 6).astype(i32)
    padding = (within(slot, SLOT) == parts) & (place < 3 * parts)
    target = jnp.where(padding, core * parts + part, 16)
    pick_ref[2 * parts * groups :, :] = (row == target).astype(bf16)


def find_held(requests, kept):
    groups = requests.shape[0]
    mine = over(requests, kept) == lax.axis_index("rep")
    held = jnp.sum(jnp.where(mine, within(requests, kept), 0), axis=1, keepdims=True)
    held = jnp.broadcast_to(held.astype(f32), (groups, LANES)).astype(bf16)
    turn = within(iota((groups, groups), 0) + TURN, groups) == iota((groups, groups), 1)
    return mm(turn.astype(bf16), held).astype(i32)


def halves(values, first):
    width = values.shape[1] // 2
    low, high = values[:, :width], values[:, width:]
    return jnp.where(first, low, high), jnp.where(first, high, low)


def products(wide, kept, held, scale, weights, message_ref, arrived=lambda piece: None):
    weight, adapters, other_weight, other_adapters = weights
    count, chip_width = wide.shape
    rank_cols = adapters.shape[0] // 2
    rank = rank_cols // kept
    chips = message_ref.shape[0]
    mine, other = halves((wide * scale).astype(bf16), lax.axis_index("c") == 0)
    squares = jnp.sum(wide * wide, axis=1, keepdims=True)
    top = squares.astype(bf16).astype(f32)
    lane = iota((count, LANES), 1)
    fold = within(iota((rank_cols, LANES), 0), rank) == iota((rank_cols, LANES), 1)
    owned = over(iota((count, rank_cols), 1), rank) == held[:, :1]
    other_ranks = mm_t(other, other_adapters[:rank_cols])
    sums = []
    for place in range(chips):
        chip = within(place + TURN_Y, chips)
        cols = pl.ds(chip * chip_width, chip_width)
        sums.append(mm(other, other_weight[:, cols]))
    for place in range(chips):
        chip = within(place + TURN_Y, chips)
        cols = pl.ds(chip * chip_width, chip_width)
        arrived(chip)
        message_ref[place, :, :chip_width] = (sums[place] + mm(mine, weight[:, cols])).astype(bf16)
    arrived(chips)
    ranks = (other_ranks + mm_t(mine, adapters[:rank_cols])).astype(bf16)
    ranks = jnp.where(owned, ranks, 0).astype(bf16)
    extra = mm(ranks, fold.astype(bf16))
    extra = jnp.where(lane == rank, top, extra)
    extra = jnp.where(lane == rank + 1, squares - top, extra).astype(bf16)
    for place in range(chips):
        message_ref[place, :, chip_width:] = extra


def update(wide, kept, held, got_ref, adapters, other_adapters):
    count, chip_width = wide.shape
    rank_cols = adapters.shape[0] // 2
    rank = rank_cols // kept
    chips = got_ref.shape[0]
    total = got_ref[0].astype(f32)
    for chip in range(1, chips):
        total += got_ref[chip].astype(f32)
    extra = total[:, chip_width:]
    lane = iota((count, LANES), 1)
    is_square = (lane == rank) | (lane == rank + 1)
    mean = jnp.sum(jnp.where(is_square, extra, 0.0), axis=1, keepdims=True) / (chip_width * chips)
    factor = lax.rsqrt(mean + EPSILON)
    ranks = jnp.where(lane < rank, extra * factor, 0.0).astype(bf16)
    unfold = within(iota((LANES, rank_cols), 1), rank) == iota((LANES, rank_cols), 0)
    spread = mm(ranks, unfold.astype(bf16))
    owned = over(iota((count, rank_cols), 1), rank) == held[:, :1]
    spread = jnp.where(owned, spread, 0.0).astype(bf16)
    first = lax.axis_index("c") == 0
    mine, other = mm(spread, adapters[rank_cols:]), mm(spread, other_adapters[rank_cols:])
    delta = [jnp.where(first, mine, other), jnp.where(first, other, mine)]
    delta = jnp.concatenate(delta, axis=1).astype(bf16).astype(f32)
    return (wide + total[:, :chip_width] * factor + delta).astype(bf16)


def first_products(kept, x_ref, pick_ref, other_weight, other_adapters, *refs):
    weight_hbm, adapters_hbm, requests_hbm = refs[:3]
    message_ref, wide_ref, scale_ref, held_ref, weight, adapters, requests_ref, sems = refs[3:]
    groups, chip_width = wide_ref.shape
    chips = message_ref.shape[0]
    copies = []
    for place in range(chips):
        cols = pl.ds(within(place + TURN_Y, chips) * chip_width, chip_width)
        copies.append((weight_hbm.at[:, cols], weight.at[:, cols]))
    copies += [(adapters_hbm, adapters), (requests_hbm, requests_ref)]
    copies = [
        pltpu.make_async_copy(source, target, sems.at[index])
        for index, (source, target) in enumerate(copies)
    ]
    for copy in copies[-1:] + copies[:-1]:
        copy.start()

    def arrived(piece):
        copies[piece if piece == chips else within(piece + chips - TURN_Y, chips)].wait()

    rows = mm(pick_ref[...], x_ref[...])
    parts = 2 * (SLOT - 1)
    wide = jnp.concatenate(
        [rows[index * groups : (index + 1) * groups] for index in range(parts)], axis=1
    )
    start = parts * groups
    scale = jnp.concatenate(
        [rows[start + index : start + index + 1] for index in range(parts)], axis=1
    )
    wide_ref[...] = wide.astype(bf16)
    scale_ref[...] = scale
    copies[-1].wait()
    held = find_held(requests_ref[...], kept)
    held_ref[...] = held
    weights = weight, adapters, other_weight, other_adapters
    products(wide, kept, held, scale, weights, message_ref, arrived)


def next_products(kept, wide_ref, got_ref, held_ref, scale_ref, *refs):
    weights, (message_ref, state_ref) = refs[:4], refs[4:]
    held = held_ref[...]
    state = update(wide_ref[...].astype(f32), kept, held, got_ref, weights[1], weights[3])
    state_ref[...] = state
    products(state.astype(f32), kept, held, scale_ref[...], weights, message_ref)


def last_update(kept, state_ref, got_ref, held_ref, adapters, other_adapters, back_ref):
    rows, cols = back_ref.shape
    width = cols // DRAFT
    old = state_ref[...]
    new = update(old.astype(f32), kept, held_ref[...], got_ref, adapters, other_adapters)
    row, place = iota((rows // 2, rows), 0), iota((rows // 2, rows), 1)
    picks = [(place == 2 * row + core).astype(bf16) for core in range(2)]
    for step, state in enumerate((old, new)):
        back_ref[:, step * width : (step + 1) * width] = sum(
            t_mm(pick, state[:, core * width : (core + 1) * width])
            for core, pick in enumerate(picks)
        ).astype(bf16)


def call(kernel, outs, operands, far=0, **kwargs):
    spaces = [pltpu.VMEM] * (len(operands) - far) + [pltpu.HBM] * far
    return pl.pallas_call(
        kernel,
        out_shape=outs,
        in_specs=[pl.BlockSpec(memory_space=space) for space in spaces],
        out_specs=[
            pl.BlockSpec(memory_space=getattr(out, "memory_space", pltpu.VMEM)) for out in outs
        ],
        compiler_params=pltpu.CompilerParams(vmem_limit_bytes=24 * 2**20),
        **kwargs,
    )(*map(pltpu.with_memory_space_constraint, operands, spaces))


def shards(first_hidden_rows, norm_scale, projection_weight, down_weights, up_weights, requests):
    groups = lax.axis_size("rep")
    chips = lax.axis_size("y")
    cores = lax.axis_size("c")
    rows, width = first_hidden_rows.shape
    chip_width = width * cores
    kept, _, rank = down_weights.shape
    rank_cols = kept * rank

    def resident(shape, dtype=bf16):
        return pltpu.VMEM(shape, dtype)

    down = jnp.transpose(down_weights, (0, 2, 1)).reshape(rank_cols, width)
    up = up_weights.reshape(rank_cols, width)
    sent, adapters = call(
        functools.partial(permute_in, kept),
        [resident((SLOT * rows, LANES)), pltpu.HBM((2 * rank_cols, width), bf16)],
        [requests, first_hidden_rows, norm_scale.reshape(-1, LANES), down, up],
        far=5,
        scratch_shapes=[
            pltpu.VMEM(requests.shape, i32),
            pltpu.VMEM((rows, width), bf16),
            pltpu.VMEM((width // LANES, LANES), f32),
            pltpu.SemaphoreType.DMA((5,)),
        ],
    )
    movers = [[(place + TURN * cores) % rows for place in range(rows)]]
    adders = [[(place + TURN_Y) % chips for place in range(chips)]]

    def move(value):
        return lax.all_to_all(
            value, ("rep", "c"), split_axis=0, concat_axis=0, axis_index_groups=movers, tiled=True
        )

    def exchange(message):
        return lax.all_to_all(
            message, "y", split_axis=0, concat_axis=0, axis_index_groups=adders, tiled=True
        )

    got = move(sent.reshape(rows, SLOT, LANES)).reshape(SLOT * rows, LANES)

    sibling = [(core, cores - 1 - core) for core in range(cores)]
    other_weight, other_adapters = (
        lax.ppermute(value, "c", sibling) for value in (projection_weight, adapters)
    )
    (picks,) = call(
        unpack_picks,
        [resident((2 * (SLOT - 1) * groups + 16, SLOT * rows))],
        [],
        cost_estimate=pl.CostEstimate(flops=HINT, bytes_accessed=0, transcendentals=0),
    )

    message_shape = resident((chips, groups, chip_width + LANES))
    state_shape = resident((groups, chip_width))
    message, wide, scale, held, weight, adapters = call(
        functools.partial(first_products, kept),
        [
            message_shape,
            state_shape,
            resident((1, chip_width), f32),
            resident((groups, LANES), i32),
            resident(projection_weight.shape),
            resident(adapters.shape),
        ],
        [got, picks, other_weight, other_adapters, projection_weight, adapters, requests],
        far=3,
        scratch_shapes=[
            pltpu.VMEM(requests.shape, i32),
            pltpu.SemaphoreType.DMA((chips + 2,)),
        ],
    )
    weights = [weight, adapters, other_weight, other_adapters]
    message, state = call(
        functools.partial(next_products, kept),
        [message_shape, state_shape],
        [wide, exchange(message), held, scale] + weights,
    )
    (back,) = call(
        functools.partial(last_update, kept),
        [resident((rows, DRAFT * width))],
        [state, exchange(message), held, adapters, other_adapters],
    )
    home = move(back.reshape(rows, DRAFT, width)).reshape(rows, DRAFT * width)
    (result,) = call(
        functools.partial(permute_out, kept),
        [jax.ShapeDtypeStruct((DRAFT, rows, width), bf16)],
        [requests, home],
    )
    return result


def solution(mesh):
    chip_mesh = Mesh(mesh.devices.reshape(mesh.shape["rep"], -1, 2), ("rep", "y", "c"))
    tp = ("y", "c")
    return jax.shard_map(
        shards,
        mesh=chip_mesh,
        in_specs=(
            P("rep", tp),
            P(tp),
            P(tp, None),
            P("rep", tp, None),
            P("rep", None, tp),
            P(),
        ),
        out_specs=P(None, "rep", tp),
        check_vma=False,
    )
```

```python
import functools

import jax
import jax.numpy as jnp
from jax import lax
from jax.experimental import pallas as pl
from jax.experimental.pallas import tpu as pltpu
from jax.sharding import Mesh, PartitionSpec as P

DRAFT = 2
LANES = 128
EPSILON = 1e-06
TURN = 34
TURN_Y = 2
HINT = 2 * 10**11
SLOT = 4

bf16, f32, i32 = jnp.bfloat16, jnp.float32, jnp.int32


def iota(shape, dim):
    return lax.broadcasted_iota(i32, shape, dim)


def over(values, size):
    return values >> (size.bit_length() - 1)


def within(values, size):
    return values & (size - 1)


def mm(left, right):
    return jnp.dot(left, right, preferred_element_type=f32)


def mm_t(left, right):
    return lax.dot_general(left, right, (((1,), (1,)), ((), ())), preferred_element_type=f32)


def t_mm(left, right):
    return lax.dot_general(left, right, (((0,), (0,)), ((), ())), preferred_element_type=f32)


def holder_places(my_requests, kept):
    blocks = my_requests.shape[1]
    return within(over(my_requests, kept) + (blocks - TURN), blocks)


def split(values):
    high = values.astype(bf16).astype(f32)
    middle = (values - high).astype(bf16).astype(f32)
    return high, middle, values - high - middle


def permute_in(kept, requests_hbm, x_hbm, scale_hbm, sent_ref, requests_ref, x_ref, scale_ref, sems):
    copies = [
        pltpu.make_async_copy(source, target, sems.at[index])
        for index, (source, target) in enumerate(
            ((x_hbm, x_ref), (requests_hbm, requests_ref), (scale_hbm, scale_ref))
        )
    ]
    for copy in copies:
        copy.start()
    me = lax.axis_index("rep")
    blocks = requests_ref.shape[1]
    rows, width = x_ref.shape
    slots = sent_ref.shape[0]
    parts = width // LANES
    row_picks = [
        (iota((blocks, rows), 1) == 2 * iota((blocks, rows), 0) + half).astype(bf16)
        for half in range(2)
    ]
    index = iota((1, 2 * parts * blocks), 1)
    piece, block = over(index, blocks), within(index, blocks)
    slot = 2 * SLOT * block + jnp.where(piece < parts, piece, SLOT + piece - parts)
    lay_out = (iota((slots, 2 * parts * blocks), 0) == slot).astype(bf16)
    padding = within(iota((slots, 1), 0), SLOT) == parts
    copies[0].wait()
    halves = [mm(pick, x_ref[...]).astype(bf16) for pick in row_picks]
    copies[1].wait()
    places = holder_places(requests_ref[pl.ds(me, 1), :], kept)
    pick = (places == iota((blocks, blocks), 0)).astype(bf16)
    picked = [mm(pick, half).astype(bf16) for half in halves]
    stacked = jnp.concatenate(
        [half[:, part * LANES : (part + 1) * LANES] for half in picked for part in range(parts)]
    )
    copies[2].wait()
    wanted = lax.rem(within(me + (blocks - TURN), blocks), 3 * parts)
    gain = jnp.zeros((1, LANES), f32)
    for part in range(parts):
        for number, value in enumerate(split(scale_ref[part : part + 1, :])):
            gain = jnp.where(wanted == 3 * part + number, value, gain)
    sent_ref[...] = jnp.where(padding, gain, mm(lay_out, stacked)).astype(bf16)


def permute_out(kept, requests_ref, home_ref, out_ref):
    me = lax.axis_index("rep")
    blocks = requests_ref.shape[1]
    rows, width = out_ref.shape[1:]
    repeat = (over(iota((blocks, rows), 1), 2) == iota((blocks, rows), 0)).astype(bf16)
    places = holder_places(requests_ref[pl.ds(me, 1), :], kept)
    places = jnp.broadcast_to(places.astype(f32), (8, blocks)).astype(bf16)
    target = mm(places, repeat)[:1].astype(i32) * 2 + within(iota((1, rows), 1), 2)
    pick = (target == iota((rows, rows), 0)).astype(bf16)
    for step in range(DRAFT):
        out_ref[step] = t_mm(pick, home_ref[:, step * width : (step + 1) * width]).astype(bf16)


def unpack_picks(pick_ref):
    slots = pick_ref.shape[1]
    groups = over(slots, 2 * SLOT)
    parts = SLOT - 1
    row, slot = iota((groups, slots), 0), iota((groups, slots), 1)
    for core in range(2):
        for part in range(parts):
            start = (core * parts + part) * groups
            hit = slot == (2 * row + core) * SLOT + part
            pick_ref[start : start + groups, :] = hit.astype(bf16)
    row, slot = iota((16, slots), 0), iota((1, slots), 1)
    place, core = over(slot, 2 * SLOT), within(over(slot, SLOT), 2)
    part = (place >= 3).astype(i32) + (place >= 6).astype(i32)
    padding = (within(slot, SLOT) == parts) & (place < 3 * parts)
    target = jnp.where(padding, core * parts + part, 16)
    pick_ref[2 * parts * groups :, :] = (row == target).astype(bf16)


def pack(after_ref, down_hbm, up_hbm, out_ref, sems):
    rank_cols = down_hbm.shape[0]
    copies = [
        pltpu.make_async_copy(down_hbm, out_ref.at[:rank_cols], sems.at[0]),
        pltpu.make_async_copy(up_hbm, out_ref.at[rank_cols:], sems.at[1]),
    ]
    for copy in copies:
        copy.start()
    for copy in copies:
        copy.wait()


def find_held(requests, kept):
    groups = requests.shape[0]
    mine = over(requests, kept) == lax.axis_index("rep")
    held = jnp.sum(jnp.where(mine, within(requests, kept), 0), axis=1, keepdims=True)
    held = jnp.broadcast_to(held.astype(f32), (groups, LANES)).astype(bf16)
    turn = within(iota((groups, groups), 0) + TURN, groups) == iota((groups, groups), 1)
    return mm(turn.astype(bf16), held).astype(i32)


def products(wide, kept, held, scale, weight, adapters, message_ref, arrived=lambda piece: None):
    count, chip_width = wide.shape
    rank_cols = adapters.shape[0] // 2
    rank = rank_cols // kept
    chips = message_ref.shape[0]
    scaled = (wide * scale).astype(bf16)
    squares = jnp.sum(wide * wide, axis=1, keepdims=True)
    top = squares.astype(bf16).astype(f32)
    lane = iota((count, LANES), 1)
    fold = within(iota((rank_cols, LANES), 0), rank) == iota((rank_cols, LANES), 1)
    owned = over(iota((count, rank_cols), 1), rank) == held[:, :1]
    arrived(0)
    ranks = mm_t(scaled, adapters[:rank_cols]).astype(bf16)
    ranks = jnp.where(owned, ranks, 0).astype(bf16)
    extra = mm(ranks, fold.astype(bf16))
    extra = jnp.where(lane == rank, top, extra)
    extra = jnp.where(lane == rank + 1, squares - top, extra).astype(bf16)
    for place in range(chips):
        arrived(1 + place)
        chip = within(place + TURN_Y, chips)
        message_ref[place, :, :chip_width] = mm(
            scaled, weight[:, chip * chip_width : (chip + 1) * chip_width]
        ).astype(bf16)
        message_ref[place, :, chip_width:] = extra


def update(wide, kept, held, got_ref, adapters):
    count, chip_width = wide.shape
    rank_cols = adapters.shape[0] // 2
    rank = rank_cols // kept
    chips = got_ref.shape[0]
    total = got_ref[0].astype(f32)
    for chip in range(1, chips):
        total += got_ref[chip].astype(f32)
    extra = total[:, chip_width:]
    lane = iota((count, LANES), 1)
    is_square = (lane == rank) | (lane == rank + 1)
    mean = jnp.sum(jnp.where(is_square, extra, 0.0), axis=1, keepdims=True) / (chip_width * chips)
    factor = lax.rsqrt(mean + EPSILON)
    ranks = jnp.where(lane < rank, extra * factor, 0.0).astype(bf16)
    unfold = within(iota((LANES, rank_cols), 1), rank) == iota((LANES, rank_cols), 0)
    spread = mm(ranks, unfold.astype(bf16))
    owned = over(iota((count, rank_cols), 1), rank) == held[:, :1]
    spread = jnp.where(owned, spread, 0.0).astype(bf16)
    delta = mm(spread, adapters[rank_cols:]).astype(bf16).astype(f32)
    return (wide + total[:, :chip_width] * factor + delta).astype(bf16)


def first_products(kept, x_ref, pick_ref, *refs):
    weights, (down, others, up, requests_hbm) = refs[:2], refs[2:6]
    message_ref, wide_ref, scale_ref, held_ref, weight_out, adapters_out, requests_ref, sems = refs[6:]
    groups, chip_width = wide_ref.shape
    width = chip_width // 2
    rank_cols = adapters_out.shape[0] // 2
    chips = message_ref.shape[0]
    core = lax.axis_index("c")
    places = [
        pl.ds(pl.multiple_of(jnp.where(core == index, 0, width), LANES), width)
        for index in range(2)
    ]
    pieces = [[] for _ in range(chips + 3)]

    def add(piece, source, target):
        copy = pltpu.make_async_copy(source, target, sems.at[sum(map(len, pieces))])
        copy.start()
        pieces[piece].append(copy)

    def arrived(piece):
        for copy in pieces[piece]:
            copy.wait()

    add(chips + 2, requests_hbm, requests_ref)
    for index in range(2):
        source = (down, others.at[:rank_cols])[index]
        add(0, source, adapters_out.at[:rank_cols, places[index]])
    for place in range(chips):
        cols = pl.ds(within(place + TURN_Y, chips) * chip_width, chip_width)
        for index in range(2):
            add(1 + place, weights[index].at[:, cols], weight_out.at[places[index], cols])
    for index in range(2):
        source = (up, others.at[rank_cols:])[index]
        add(chips + 1, source, adapters_out.at[rank_cols:, places[index]])

    rows = mm(pick_ref[...], x_ref[...])
    parts = 2 * (SLOT - 1)
    wide = jnp.concatenate(
        [rows[index * groups : (index + 1) * groups] for index in range(parts)], axis=1
    )
    start = parts * groups
    scale = jnp.concatenate(
        [rows[start + index : start + index + 1] for index in range(parts)], axis=1
    )
    wide_ref[...] = wide.astype(bf16)
    scale_ref[...] = scale
    arrived(chips + 2)
    held = find_held(requests_ref[...], kept)
    held_ref[...] = held
    products(wide, kept, held, scale, weight_out, adapters_out, message_ref, arrived)
    arrived(chips + 1)


def next_products(kept, wide_ref, got_ref, held_ref, scale_ref, weight, adapters, message_ref, state_ref):
    held = held_ref[...]
    state = update(wide_ref[...].astype(f32), kept, held, got_ref, adapters)
    state_ref[...] = state
    products(state.astype(f32), kept, held, scale_ref[...], weight, adapters, message_ref)


def last_update(kept, state_ref, got_ref, held_ref, adapters, back_ref):
    rows, cols = back_ref.shape
    width = cols // DRAFT
    old = state_ref[...]
    new = update(old.astype(f32), kept, held_ref[...], got_ref, adapters)
    row, place = iota((rows // 2, rows), 0), iota((rows // 2, rows), 1)
    picks = [(place == 2 * row + core).astype(bf16) for core in range(2)]
    for step, state in enumerate((old, new)):
        back_ref[:, step * width : (step + 1) * width] = sum(
            t_mm(pick, state[:, core * width : (core + 1) * width])
            for core, pick in enumerate(picks)
        ).astype(bf16)


def call(kernel, outs, operands, far=0, loose=(), **kwargs):
    spaces = [pltpu.VMEM] * (len(operands) - far) + [pltpu.HBM] * far
    for index in loose:
        spaces[index] = pl.ANY
    return pl.pallas_call(
        kernel,
        out_shape=outs,
        in_specs=[pl.BlockSpec(memory_space=space) for space in spaces],
        out_specs=[
            pl.BlockSpec(memory_space=getattr(out, "memory_space", pltpu.VMEM)) for out in outs
        ],
        compiler_params=pltpu.CompilerParams(vmem_limit_bytes=24 * 2**20),
        **kwargs,
    )(*map(pltpu.with_memory_space_constraint, operands, spaces))


def shards(first_hidden_rows, norm_scale, projection_weight, down_weights, up_weights, requests):
    groups = lax.axis_size("rep")
    chips = lax.axis_size("y")
    cores = lax.axis_size("c")
    rows, width = first_hidden_rows.shape
    chip_width = width * cores
    kept, _, rank = down_weights.shape
    rank_cols = kept * rank

    def resident(shape, dtype=bf16):
        return pltpu.VMEM(shape, dtype)

    (sent,) = call(
        functools.partial(permute_in, kept),
        [resident((SLOT * rows, LANES))],
        [requests, first_hidden_rows, norm_scale.reshape(-1, LANES)],
        far=3,
        scratch_shapes=[
            pltpu.VMEM(requests.shape, i32),
            pltpu.VMEM((rows, width), bf16),
            pltpu.VMEM((width // LANES, LANES), f32),
            pltpu.SemaphoreType.DMA((3,)),
        ],
    )
    movers = [[(place + TURN * cores) % rows for place in range(rows)]]
    adders = [[(place + TURN_Y) % chips for place in range(chips)]]

    def move(value):
        return lax.all_to_all(
            value, ("rep", "c"), split_axis=0, concat_axis=0, axis_index_groups=movers, tiled=True
        )

    def exchange(message):
        return lax.all_to_all(
            message, "y", split_axis=0, concat_axis=0, axis_index_groups=adders, tiled=True
        )

    got = move(sent.reshape(rows, SLOT, LANES)).reshape(SLOT * rows, LANES)

    (picks,) = call(
        unpack_picks,
        [resident((2 * (SLOT - 1) * groups + 16, SLOT * rows))],
        [],
        cost_estimate=pl.CostEstimate(flops=HINT, bytes_accessed=0, transcendentals=0),
    )
    down = jnp.transpose(down_weights, (0, 2, 1)).reshape(rank_cols, width)
    up = up_weights.reshape(rank_cols, width)
    (adapters,) = call(
        pack,
        [resident((2 * rank_cols, width))],
        [picks, down, up],
        far=2,
        scratch_shapes=[pltpu.SemaphoreType.DMA((2,))],
    )
    sibling = [(core, cores - 1 - core) for core in range(cores)]
    other_weight, other_adapters = (
        lax.ppermute(value, "c", sibling) for value in (projection_weight, adapters)
    )

    message_shape = resident((chips, groups, chip_width + LANES))
    state_shape = resident((groups, chip_width))
    message, wide, scale, held, weight, adapters = call(
        functools.partial(first_products, kept),
        [
            message_shape,
            state_shape,
            resident((1, chip_width), f32),
            resident((groups, LANES), i32),
            resident((chip_width, projection_weight.shape[1])),
            resident((2 * rank_cols, chip_width)),
        ],
        [got, picks, projection_weight, other_weight, down, other_adapters, up, requests],
        far=6,
        loose=(3, 5),
        scratch_shapes=[
            pltpu.VMEM(requests.shape, i32),
            pltpu.SemaphoreType.DMA((2 * chips + 5,)),
        ],
    )
    message, state = call(
        functools.partial(next_products, kept),
        [message_shape, state_shape],
        [wide, exchange(message), held, scale, weight, adapters],
    )
    (back,) = call(
        functools.partial(last_update, kept),
        [resident((rows, DRAFT * width))],
        [state, exchange(message), held, adapters],
    )
    home = move(back.reshape(rows, DRAFT, width)).reshape(rows, DRAFT * width)
    (result,) = call(
        functools.partial(permute_out, kept),
        [jax.ShapeDtypeStruct((DRAFT, rows, width), bf16)],
        [requests, home],
    )
    return result


def solution(mesh):
    chip_mesh = Mesh(mesh.devices.reshape(mesh.shape["rep"], -1, 2), ("rep", "y", "c"))
    tp = ("y", "c")
    return jax.shard_map(
        shards,
        mesh=chip_mesh,
        in_specs=(
            P("rep", tp),
            P(tp),
            P(tp, None),
            P("rep", tp, None),
            P("rep", None, tp),
            P(),
        ),
        out_specs=P(None, "rep", tp),
        check_vma=False,
    )
```

```python
import functools

import jax
import jax.numpy as jnp
from jax import lax
from jax.experimental import pallas as pl
from jax.experimental.pallas import tpu as pltpu
from jax.sharding import Mesh, PartitionSpec as P

DRAFT = 2
LANES = 128
EPSILON = 1e-06
TURN = 34
TURN_Y = 2
HINT = 2 * 10**11
SLOT = 4

bf16, f32, i32 = jnp.bfloat16, jnp.float32, jnp.int32


def iota(shape, dim):
    return lax.broadcasted_iota(i32, shape, dim)


def over(values, size):
    return values >> (size.bit_length() - 1)


def within(values, size):
    return values & (size - 1)


def mm(left, right):
    return jnp.dot(left, right, preferred_element_type=f32)


def mm_t(left, right):
    return lax.dot_general(left, right, (((1,), (1,)), ((), ())), preferred_element_type=f32)


def t_mm(left, right):
    return lax.dot_general(left, right, (((0,), (0,)), ((), ())), preferred_element_type=f32)


def holder_places(my_requests, kept):
    blocks = my_requests.shape[1]
    return within(over(my_requests, kept) + (blocks - TURN), blocks)


def split(values):
    high = values.astype(bf16).astype(f32)
    middle = (values - high).astype(bf16).astype(f32)
    return high, middle, values - high - middle


def permute_in(kept, requests_hbm, x_hbm, scale_hbm, sent_ref, requests_ref, x_ref, scale_ref, sems):
    copies = [
        pltpu.make_async_copy(source, target, sems.at[index])
        for index, (source, target) in enumerate(
            ((x_hbm, x_ref), (requests_hbm, requests_ref), (scale_hbm, scale_ref))
        )
    ]
    for copy in copies:
        copy.start()
    me = lax.axis_index("rep")
    blocks = requests_ref.shape[1]
    rows, width = x_ref.shape
    slots = sent_ref.shape[0]
    parts = width // LANES
    row_picks = [
        (iota((blocks, rows), 1) == 2 * iota((blocks, rows), 0) + half).astype(bf16)
        for half in range(2)
    ]
    index = iota((1, 2 * parts * blocks), 1)
    piece, block = over(index, blocks), within(index, blocks)
    slot = 2 * SLOT * block + jnp.where(piece < parts, piece, SLOT + piece - parts)
    lay_out = (iota((slots, 2 * parts * blocks), 0) == slot).astype(bf16)
    padding = within(iota((slots, 1), 0), SLOT) == parts
    copies[0].wait()
    halves = [mm(pick, x_ref[...]).astype(bf16) for pick in row_picks]
    copies[1].wait()
    places = holder_places(requests_ref[pl.ds(me, 1), :], kept)
    pick = (places == iota((blocks, blocks), 0)).astype(bf16)
    picked = [mm(pick, half).astype(bf16) for half in halves]
    stacked = jnp.concatenate(
        [half[:, part * LANES : (part + 1) * LANES] for half in picked for part in range(parts)]
    )
    copies[2].wait()
    wanted = lax.rem(within(me + (blocks - TURN), blocks), 3 * parts)
    gain = jnp.zeros((1, LANES), f32)
    for part in range(parts):
        for number, value in enumerate(split(scale_ref[part : part + 1, :])):
            gain = jnp.where(wanted == 3 * part + number, value, gain)
    sent_ref[...] = jnp.where(padding, gain, mm(lay_out, stacked)).astype(bf16)


def permute_out(kept, requests_ref, home_ref, out_ref):
    me = lax.axis_index("rep")
    blocks = requests_ref.shape[1]
    rows, width = out_ref.shape[1:]
    repeat = (over(iota((blocks, rows), 1), 2) == iota((blocks, rows), 0)).astype(bf16)
    places = holder_places(requests_ref[pl.ds(me, 1), :], kept)
    places = jnp.broadcast_to(places.astype(f32), (8, blocks)).astype(bf16)
    target = mm(places, repeat)[:1].astype(i32) * 2 + within(iota((1, rows), 1), 2)
    pick = (target == iota((rows, rows), 0)).astype(bf16)
    for step in range(DRAFT):
        out_ref[step] = t_mm(pick, home_ref[:, step * width : (step + 1) * width]).astype(bf16)


def unpack_picks(groups):
    slots, parts = 2 * SLOT * groups, SLOT - 1
    row, slot = iota((groups, slots), 0), iota((groups, slots), 1)
    picks = [
        (slot == (2 * row + core) * SLOT + part).astype(bf16)
        for core in range(2)
        for part in range(parts)
    ]
    row, slot = iota((16, slots), 0), iota((1, slots), 1)
    place, core = over(slot, 2 * SLOT), within(over(slot, SLOT), 2)
    part = (place >= 3).astype(i32) + (place >= 6).astype(i32)
    padding = (within(slot, SLOT) == parts) & (place < 3 * parts)
    picks.append((row == jnp.where(padding, core * parts + part, 16)).astype(bf16))
    return jnp.concatenate(picks)


def pack(down_hbm, up_hbm, out_ref, sems):
    rank_cols = down_hbm.shape[0]
    copies = [
        pltpu.make_async_copy(down_hbm, out_ref.at[:rank_cols], sems.at[0]),
        pltpu.make_async_copy(up_hbm, out_ref.at[rank_cols:], sems.at[1]),
    ]
    for copy in copies:
        copy.start()
    for copy in copies:
        copy.wait()


def find_held(requests, kept):
    groups = requests.shape[0]
    mine = over(requests, kept) == lax.axis_index("rep")
    held = jnp.sum(jnp.where(mine, within(requests, kept), 0), axis=1, keepdims=True)
    held = jnp.broadcast_to(held.astype(f32), (groups, LANES)).astype(bf16)
    turn = within(iota((groups, groups), 0) + TURN, groups) == iota((groups, groups), 1)
    return mm(turn.astype(bf16), held).astype(i32)


def products(wide, kept, held, scale, weights, adapters, message_ref, arrived=lambda chip: None):
    count, chip_width = wide.shape
    rank_cols = adapters.shape[0] // 2
    rank = rank_cols // kept
    chips = message_ref.shape[0]
    scaled = (wide * scale).astype(bf16)
    squares = jnp.sum(wide * wide, axis=1, keepdims=True)
    top = squares.astype(bf16).astype(f32)
    lane = iota((count, LANES), 1)
    fold = within(iota((rank_cols, LANES), 0), rank) == iota((rank_cols, LANES), 1)
    owned = over(iota((count, rank_cols), 1), rank) == held[:, :1]
    ranks = mm_t(scaled, adapters[:rank_cols]).astype(bf16)
    ranks = jnp.where(owned, ranks, 0).astype(bf16)
    extra = mm(ranks, fold.astype(bf16))
    extra = jnp.where(lane == rank, top, extra)
    extra = jnp.where(lane == rank + 1, squares - top, extra).astype(bf16)
    staged, loaded = weights
    for chip in range(chips):
        place = within(chip + chips - TURN_Y, chips)
        start = chip * chip_width
        weight = staged
        if start >= staged.shape[1]:
            start -= staged.shape[1]
            weight = loaded
            arrived(start // chip_width)
        message_ref[place, :, :chip_width] = mm(
            scaled, weight[:, start : start + chip_width]
        ).astype(bf16)
        message_ref[place, :, chip_width:] = extra


def update(wide, kept, held, got_ref, adapters):
    count, chip_width = wide.shape
    rank_cols = adapters.shape[0] // 2
    rank = rank_cols // kept
    chips = got_ref.shape[0]
    total = got_ref[0].astype(f32)
    for chip in range(1, chips):
        total += got_ref[chip].astype(f32)
    extra = total[:, chip_width:]
    lane = iota((count, LANES), 1)
    is_square = (lane == rank) | (lane == rank + 1)
    mean = jnp.sum(jnp.where(is_square, extra, 0.0), axis=1, keepdims=True) / (chip_width * chips)
    factor = lax.rsqrt(mean + EPSILON)
    ranks = jnp.where(lane < rank, extra * factor, 0.0).astype(bf16)
    unfold = within(iota((LANES, rank_cols), 1), rank) == iota((LANES, rank_cols), 0)
    spread = mm(ranks, unfold.astype(bf16))
    owned = over(iota((count, rank_cols), 1), rank) == held[:, :1]
    spread = jnp.where(owned, spread, 0.0).astype(bf16)
    delta = mm(spread, adapters[rank_cols:]).astype(bf16).astype(f32)
    return (wide + total[:, :chip_width] * factor + delta).astype(bf16)


def stage(kept, weight, other_weight, down, others, up, requests_hbm, *refs):
    weight_out, adapters_out, held_ref, requests_ref, sems = refs
    width = adapters_out.shape[1] // 2
    rank_cols = adapters_out.shape[0] // 2
    core = lax.axis_index("c")
    copies = [(requests_hbm, requests_ref)]
    for index in range(2):
        place = pl.ds(pl.multiple_of(jnp.where(core == index, 0, width), LANES), width)
        copies += [
            ((down, others.at[:rank_cols])[index], adapters_out.at[:rank_cols, place]),
            ((up, others.at[rank_cols:])[index], adapters_out.at[rank_cols:, place]),
        ]
        for chip in range(weight_out.shape[1] // (2 * width)):
            cols = pl.ds(chip * 2 * width, 2 * width)
            source = (weight, other_weight)[index]
            copies.append((source.at[:, cols], weight_out.at[place, cols]))
    copies = [
        pltpu.make_async_copy(source, target, sems.at[index])
        for index, (source, target) in enumerate(copies)
    ]
    for copy in copies:
        copy.start()
    copies[0].wait()
    held_ref[...] = find_held(requests_ref[...], kept)
    for copy in copies[1:]:
        copy.wait()


def first_products(kept, held_ref, staged, adapters, x_hbm, weight, other_weight, *refs):
    message_ref, wide_ref, scale_ref, loaded, x_ref, sems = refs
    groups, chip_width = wide_ref.shape
    width = chip_width // 2
    core = lax.axis_index("c")
    copies = [pltpu.make_async_copy(x_hbm, x_ref, sems.at[0])]
    copies[0].start()
    for chip in range(loaded.shape[1] // chip_width):
        cols = pl.ds(chip * chip_width, chip_width)
        source_cols = pl.ds(staged.shape[1] + chip * chip_width, chip_width)
        for index, source in enumerate((weight, other_weight)):
            place = pl.ds(pl.multiple_of(jnp.where(core == index, 0, width), LANES), width)
            copy = pltpu.make_async_copy(
                source.at[:, source_cols], loaded.at[place, cols], sems.at[len(copies)]
            )
            copy.start()
            copies.append(copy)

    def arrived(chip):
        for copy in copies[1 + 2 * chip : 3 + 2 * chip]:
            copy.wait()

    picks = unpack_picks(groups)
    copies[0].wait()
    rows = mm(picks, x_ref[...])
    parts = 2 * (SLOT - 1)
    wide = jnp.concatenate(
        [rows[index * groups : (index + 1) * groups] for index in range(parts)], axis=1
    )
    start = parts * groups
    scale = jnp.concatenate(
        [rows[start + index : start + index + 1] for index in range(parts)], axis=1
    )
    wide_ref[...] = wide.astype(bf16)
    scale_ref[...] = scale
    products(wide, kept, held_ref[...], scale, (staged, loaded), adapters, message_ref, arrived)


def next_products(kept, wide_ref, got_ref, held_ref, scale_ref, staged, loaded, adapters, *refs):
    message_ref, state_ref = refs
    held = held_ref[...]
    state = update(wide_ref[...].astype(f32), kept, held, got_ref, adapters)
    state_ref[...] = state
    products(state.astype(f32), kept, held, scale_ref[...], (staged, loaded), adapters, message_ref)


def last_update(kept, state_ref, got_ref, held_ref, adapters, back_ref):
    rows, cols = back_ref.shape
    width = cols // DRAFT
    old = state_ref[...]
    new = update(old.astype(f32), kept, held_ref[...], got_ref, adapters)
    row, place = iota((rows // 2, rows), 0), iota((rows // 2, rows), 1)
    picks = [(place == 2 * row + core).astype(bf16) for core in range(2)]
    for step, state in enumerate((old, new)):
        back_ref[:, step * width : (step + 1) * width] = sum(
            t_mm(pick, state[:, core * width : (core + 1) * width])
            for core, pick in enumerate(picks)
        ).astype(bf16)


def call(kernel, outs, operands, far=0, loose=(), **kwargs):
    spaces = [pltpu.VMEM] * (len(operands) - far) + [pltpu.HBM] * far
    for index in loose:
        spaces[index] = pl.ANY
    return pl.pallas_call(
        kernel,
        out_shape=outs,
        in_specs=[pl.BlockSpec(memory_space=space) for space in spaces],
        out_specs=[
            pl.BlockSpec(memory_space=getattr(out, "memory_space", pltpu.VMEM)) for out in outs
        ],
        compiler_params=pltpu.CompilerParams(vmem_limit_bytes=24 * 2**20),
        **kwargs,
    )(*map(pltpu.with_memory_space_constraint, operands, spaces))


def shards(first_hidden_rows, norm_scale, projection_weight, down_weights, up_weights, requests):
    groups = lax.axis_size("rep")
    chips = lax.axis_size("y")
    cores = lax.axis_size("c")
    rows, width = first_hidden_rows.shape
    chip_width = width * cores
    kept, _, rank = down_weights.shape
    rank_cols = kept * rank

    def resident(shape, dtype=bf16):
        return pltpu.VMEM(shape, dtype)

    (sent,) = call(
        functools.partial(permute_in, kept),
        [resident((SLOT * rows, LANES))],
        [requests, first_hidden_rows, norm_scale.reshape(-1, LANES)],
        far=3,
        scratch_shapes=[
            pltpu.VMEM(requests.shape, i32),
            pltpu.VMEM((rows, width), bf16),
            pltpu.VMEM((width // LANES, LANES), f32),
            pltpu.SemaphoreType.DMA((3,)),
        ],
    )
    movers = [[(place + TURN * cores) % rows for place in range(rows)]]
    adders = [[(place + TURN_Y) % chips for place in range(chips)]]

    def move(value):
        return lax.all_to_all(
            value, ("rep", "c"), split_axis=0, concat_axis=0, axis_index_groups=movers, tiled=True
        )

    def exchange(message):
        return lax.all_to_all(
            message, "y", split_axis=0, concat_axis=0, axis_index_groups=adders, tiled=True
        )

    got = move(sent.reshape(rows, SLOT, LANES)).reshape(SLOT * rows, LANES)

    down = jnp.transpose(down_weights, (0, 2, 1)).reshape(rank_cols, width)
    up = up_weights.reshape(rank_cols, width)
    (adapters,) = call(
        pack,
        [resident((2 * rank_cols, width))],
        [down, up],
        far=2,
        scratch_shapes=[pltpu.SemaphoreType.DMA((2,))],
        cost_estimate=pl.CostEstimate(flops=HINT, bytes_accessed=0, transcendentals=0),
    )
    sibling = [(core, cores - 1 - core) for core in range(cores)]
    other_weight, other_adapters = (
        lax.ppermute(value, "c", sibling) for value in (projection_weight, adapters)
    )

    message_shape = resident((chips, groups, chip_width + LANES))
    state_shape = resident((groups, chip_width))
    half = resident((chip_width, projection_weight.shape[1] // 2))
    staged, adapters, held = call(
        functools.partial(stage, kept),
        [half, resident((2 * rank_cols, chip_width)), resident((groups, LANES), i32)],
        [projection_weight, other_weight, down, other_adapters, up, requests],
        far=6,
        loose=(1, 3),
        scratch_shapes=[pltpu.VMEM(requests.shape, i32), pltpu.SemaphoreType.DMA((chips + 5,))],
    )
    message, wide, scale, loaded = call(
        functools.partial(first_products, kept),
        [message_shape, state_shape, resident((1, chip_width), f32), half],
        [held, staged, adapters, got, projection_weight, other_weight],
        far=3,
        loose=(3, 5),
        scratch_shapes=[pltpu.VMEM(got.shape, bf16), pltpu.SemaphoreType.DMA((chips + 1,))],
    )
    message, state = call(
        functools.partial(next_products, kept),
        [message_shape, state_shape],
        [wide, exchange(message), held, scale, staged, loaded, adapters],
    )
    (back,) = call(
        functools.partial(last_update, kept),
        [resident((rows, DRAFT * width))],
        [state, exchange(message), held, adapters],
    )
    home = move(back.reshape(rows, DRAFT, width)).reshape(rows, DRAFT * width)
    (result,) = call(
        functools.partial(permute_out, kept),
        [jax.ShapeDtypeStruct((DRAFT, rows, width), bf16)],
        [requests, home],
    )
    return result


def solution(mesh):
    chip_mesh = Mesh(mesh.devices.reshape(mesh.shape["rep"], -1, 2), ("rep", "y", "c"))
    tp = ("y", "c")
    return jax.shard_map(
        shards,
        mesh=chip_mesh,
        in_specs=(
            P("rep", tp),
            P(tp),
            P(tp, None),
            P("rep", tp, None),
            P("rep", None, tp),
            P(),
        ),
        out_specs=P(None, "rep", tp),
        check_vma=False,
    )
```

```python
import functools

import jax
import jax.numpy as jnp
from jax import lax
from jax.experimental import pallas as pl
from jax.experimental.pallas import tpu as pltpu
from jax.sharding import Mesh, PartitionSpec as P

DRAFT = 2
LANES = 128
EPSILON = 1e-06
TURN = 34
TURN_Y = 2
HINT = 6 * 10**10
SLOT = 4

bf16, f32, i32 = jnp.bfloat16, jnp.float32, jnp.int32


def iota(shape, dim):
    return lax.broadcasted_iota(i32, shape, dim)


def over(values, size):
    return values >> (size.bit_length() - 1)


def within(values, size):
    return values & (size - 1)


def mm(left, right):
    return jnp.dot(left, right, preferred_element_type=f32)


def mm_t(left, right):
    return lax.dot_general(left, right, (((1,), (1,)), ((), ())), preferred_element_type=f32)


def t_mm(left, right):
    return lax.dot_general(left, right, (((0,), (0,)), ((), ())), preferred_element_type=f32)


def holder_places(my_requests, kept):
    blocks = my_requests.shape[1]
    return within(over(my_requests, kept) + (blocks - TURN), blocks)


def split(values):
    high = values.astype(bf16).astype(f32)
    middle = (values - high).astype(bf16).astype(f32)
    return high, middle, values - high - middle


def permute_in(kept, requests_hbm, x_hbm, scale_hbm, down_hbm, up_hbm, *refs):
    sent_ref, adapters_ref, requests_ref, x_ref, scale_ref, sems = refs
    rank_cols = down_hbm.shape[0]
    copies = [
        pltpu.make_async_copy(source, target, sems.at[index])
        for index, (source, target) in enumerate(
            (
                (x_hbm, x_ref),
                (requests_hbm, requests_ref),
                (scale_hbm, scale_ref),
                (down_hbm, adapters_ref.at[:rank_cols]),
                (up_hbm, adapters_ref.at[rank_cols:]),
            )
        )
    ]
    for copy in copies:
        copy.start()
    me = lax.axis_index("rep")
    blocks = requests_ref.shape[1]
    rows, width = x_ref.shape
    slots = sent_ref.shape[0]
    parts = width // LANES
    row_picks = [
        (iota((blocks, rows), 1) == 2 * iota((blocks, rows), 0) + half).astype(bf16)
        for half in range(2)
    ]
    index = iota((1, 2 * parts * blocks), 1)
    piece, block = over(index, blocks), within(index, blocks)
    slot = 2 * SLOT * block + jnp.where(piece < parts, piece, SLOT + piece - parts)
    lay_out = (iota((slots, 2 * parts * blocks), 0) == slot).astype(bf16)
    padding = within(iota((slots, 1), 0), SLOT) == parts
    copies[0].wait()
    halves = [mm(pick, x_ref[...]).astype(bf16) for pick in row_picks]
    copies[1].wait()
    places = holder_places(requests_ref[pl.ds(me, 1), :], kept)
    pick = (places == iota((blocks, blocks), 0)).astype(bf16)
    picked = [mm(pick, half).astype(bf16) for half in halves]
    stacked = jnp.concatenate(
        [half[:, part * LANES : (part + 1) * LANES] for half in picked for part in range(parts)]
    )
    copies[2].wait()
    wanted = lax.rem(within(me + (blocks - TURN), blocks), 3 * parts)
    gain = jnp.zeros((1, LANES), f32)
    for part in range(parts):
        for number, value in enumerate(split(scale_ref[part : part + 1, :])):
            gain = jnp.where(wanted == 3 * part + number, value, gain)
    sent_ref[...] = jnp.where(padding, gain, mm(lay_out, stacked)).astype(bf16)
    for copy in copies[3:]:
        copy.wait()


def permute_out(kept, requests_ref, home_ref, out_ref):
    me = lax.axis_index("rep")
    blocks = requests_ref.shape[1]
    rows, width = out_ref.shape[1:]
    repeat = (over(iota((blocks, rows), 1), 2) == iota((blocks, rows), 0)).astype(bf16)
    places = holder_places(requests_ref[pl.ds(me, 1), :], kept)
    places = jnp.broadcast_to(places.astype(f32), (8, blocks)).astype(bf16)
    target = mm(places, repeat)[:1].astype(i32) * 2 + within(iota((1, rows), 1), 2)
    pick = (target == iota((rows, rows), 0)).astype(bf16)
    for step in range(DRAFT):
        out_ref[step] = t_mm(pick, home_ref[:, step * width : (step + 1) * width]).astype(bf16)


def unpack_picks(groups):
    slots, parts = 2 * SLOT * groups, SLOT - 1
    row, slot = iota((groups, slots), 0), iota((groups, slots), 1)
    picks = [
        (slot == (2 * row + core) * SLOT + part).astype(bf16)
        for core in range(2)
        for part in range(parts)
    ]
    row, slot = iota((16, slots), 0), iota((1, slots), 1)
    place, core = over(slot, 2 * SLOT), within(over(slot, SLOT), 2)
    part = (place >= 3).astype(i32) + (place >= 6).astype(i32)
    padding = (within(slot, SLOT) == parts) & (place < 3 * parts)
    picks.append((row == jnp.where(padding, core * parts + part, 16)).astype(bf16))
    return jnp.concatenate(picks)


def pass_on(value_ref, out_ref):
    out_ref[...] = value_ref[...]


def find_held(requests, kept):
    groups = requests.shape[0]
    mine = over(requests, kept) == lax.axis_index("rep")
    held = jnp.sum(jnp.where(mine, within(requests, kept), 0), axis=1, keepdims=True)
    held = jnp.broadcast_to(held.astype(f32), (groups, LANES)).astype(bf16)
    turn = within(iota((groups, groups), 0) + TURN, groups) == iota((groups, groups), 1)
    return mm(turn.astype(bf16), held).astype(i32)


def products(wide, kept, held, scale, weight, adapters, message_ref, arrived=lambda piece: None):
    count, chip_width = wide.shape
    rank_cols = adapters.shape[0] // 2
    rank = rank_cols // kept
    chips = message_ref.shape[0]
    scaled = (wide * scale).astype(bf16)
    squares = jnp.sum(wide * wide, axis=1, keepdims=True)
    top = squares.astype(bf16).astype(f32)
    lane = iota((count, LANES), 1)
    fold = within(iota((rank_cols, LANES), 0), rank) == iota((rank_cols, LANES), 1)
    owned = over(iota((count, rank_cols), 1), rank) == held[:, :1]
    arrived(chips)
    ranks = mm_t(scaled, adapters[:rank_cols]).astype(bf16)
    ranks = jnp.where(owned, ranks, 0).astype(bf16)
    extra = mm(ranks, fold.astype(bf16))
    extra = jnp.where(lane == rank, top, extra)
    extra = jnp.where(lane == rank + 1, squares - top, extra).astype(bf16)
    for chip in range(chips):
        place = within(chip + chips - TURN_Y, chips)
        arrived(chip)
        message_ref[place, :, :chip_width] = mm(
            scaled, weight[:, chip * chip_width : (chip + 1) * chip_width]
        ).astype(bf16)
        message_ref[place, :, chip_width:] = extra


def update(wide, kept, held, got_ref, adapters):
    count, chip_width = wide.shape
    rank_cols = adapters.shape[0] // 2
    rank = rank_cols // kept
    chips = got_ref.shape[0]
    total = got_ref[0].astype(f32)
    for chip in range(1, chips):
        total += got_ref[chip].astype(f32)
    extra = total[:, chip_width:]
    lane = iota((count, LANES), 1)
    is_square = (lane == rank) | (lane == rank + 1)
    mean = jnp.sum(jnp.where(is_square, extra, 0.0), axis=1, keepdims=True) / (chip_width * chips)
    factor = lax.rsqrt(mean + EPSILON)
    ranks = jnp.where(lane < rank, extra * factor, 0.0).astype(bf16)
    unfold = within(iota((LANES, rank_cols), 1), rank) == iota((LANES, rank_cols), 0)
    spread = mm(ranks, unfold.astype(bf16))
    owned = over(iota((count, rank_cols), 1), rank) == held[:, :1]
    spread = jnp.where(owned, spread, 0.0).astype(bf16)
    delta = mm(spread, adapters[rank_cols:]).astype(bf16).astype(f32)
    return (wide + total[:, :chip_width] * factor + delta).astype(bf16)


def first_products(kept, x_ref, other_weight, others, weight, down, up, requests_hbm, *refs):
    message_ref, wide_ref, scale_ref, held_ref, weight_out, adapters_out = refs[:6]
    requests_ref, sems = refs[6:]
    groups, chip_width = wide_ref.shape
    width = chip_width // 2
    rank_cols = adapters_out.shape[0] // 2
    chips = message_ref.shape[0]
    first = lax.axis_index("c") == 0
    mine = pl.ds(pl.multiple_of(jnp.where(first, 0, width), LANES), width)
    other = pl.ds(pl.multiple_of(jnp.where(first, width, 0), LANES), width)
    blocks = [pl.ds(chip * chip_width, chip_width) for chip in range(chips)]
    copies = [(weight.at[:, cols], weight_out.at[mine, cols]) for cols in blocks]
    copies += [
        (down, adapters_out.at[:rank_cols, mine]),
        (up, adapters_out.at[rank_cols:, mine]),
        (requests_hbm, requests_ref),
    ]
    copies = [
        pltpu.make_async_copy(source, target, sems.at[index])
        for index, (source, target) in enumerate(copies)
    ]
    for copy in [copies[-1], copies[chips]] + copies[:chips] + [copies[chips + 1]]:
        copy.start()

    rows = mm(unpack_picks(groups), x_ref[...])
    parts = 2 * (SLOT - 1)
    wide = jnp.concatenate(
        [rows[index * groups : (index + 1) * groups] for index in range(parts)], axis=1
    )
    start = parts * groups
    scale = jnp.concatenate(
        [rows[start + index : start + index + 1] for index in range(parts)], axis=1
    )
    wide_ref[...] = wide.astype(bf16)
    scale_ref[...] = scale
    adapters_out[:, other] = others[...]
    for cols in blocks:
        weight_out[other, cols] = other_weight[:, cols]
    copies[-1].wait()
    held = find_held(requests_ref[...], kept)
    held_ref[...] = held

    def arrived(piece):
        copies[piece].wait()

    products(wide, kept, held, scale, weight_out, adapters_out, message_ref, arrived)
    copies[chips + 1].wait()


def next_products(kept, wide_ref, got_ref, held_ref, scale_ref, weight, adapters, *refs):
    message_ref, state_ref = refs
    held = held_ref[...]
    state = update(wide_ref[...].astype(f32), kept, held, got_ref, adapters)
    state_ref[...] = state
    products(state.astype(f32), kept, held, scale_ref[...], weight, adapters, message_ref)


def last_update(kept, state_ref, got_ref, held_ref, adapters, back_ref):
    rows, cols = back_ref.shape
    width = cols // DRAFT
    old = state_ref[...]
    new = update(old.astype(f32), kept, held_ref[...], got_ref, adapters)
    row, place = iota((rows // 2, rows), 0), iota((rows // 2, rows), 1)
    picks = [(place == 2 * row + core).astype(bf16) for core in range(2)]
    for step, state in enumerate((old, new)):
        back_ref[:, step * width : (step + 1) * width] = sum(
            t_mm(pick, state[:, core * width : (core + 1) * width])
            for core, pick in enumerate(picks)
        ).astype(bf16)


def call(kernel, outs, operands, far=0, **kwargs):
    spaces = [pltpu.VMEM] * (len(operands) - far) + [pltpu.HBM] * far
    return pl.pallas_call(
        kernel,
        out_shape=outs,
        in_specs=[pl.BlockSpec(memory_space=space) for space in spaces],
        out_specs=[
            pl.BlockSpec(memory_space=getattr(out, "memory_space", pltpu.VMEM)) for out in outs
        ],
        compiler_params=pltpu.CompilerParams(vmem_limit_bytes=24 * 2**20),
        **kwargs,
    )(*map(pltpu.with_memory_space_constraint, operands, spaces))


def shards(first_hidden_rows, norm_scale, projection_weight, down_weights, up_weights, requests):
    groups = lax.axis_size("rep")
    chips = lax.axis_size("y")
    cores = lax.axis_size("c")
    rows, width = first_hidden_rows.shape
    chip_width = width * cores
    kept, _, rank = down_weights.shape
    rank_cols = kept * rank

    def resident(shape, dtype=bf16):
        return pltpu.VMEM(shape, dtype)

    down = jnp.transpose(down_weights, (0, 2, 1)).reshape(rank_cols, width)
    up = up_weights.reshape(rank_cols, width)
    sent, adapters = call(
        functools.partial(permute_in, kept),
        [resident((SLOT * rows, LANES)), resident((2 * rank_cols, width))],
        [requests, first_hidden_rows, norm_scale.reshape(-1, LANES), down, up],
        far=5,
        scratch_shapes=[
            pltpu.VMEM(requests.shape, i32),
            pltpu.VMEM((rows, width), bf16),
            pltpu.VMEM((width // LANES, LANES), f32),
            pltpu.SemaphoreType.DMA((5,)),
        ],
    )
    movers = [[(place + TURN * cores) % rows for place in range(rows)]]
    adders = [[(place + TURN_Y) % chips for place in range(chips)]]

    def move(value):
        return lax.all_to_all(
            value, ("rep", "c"), split_axis=0, concat_axis=0, axis_index_groups=movers, tiled=True
        )

    def exchange(message):
        return lax.all_to_all(
            message, "y", split_axis=0, concat_axis=0, axis_index_groups=adders, tiled=True
        )

    got = move(sent.reshape(rows, SLOT, LANES)).reshape(SLOT * rows, LANES)

    (adapters,) = call(
        pass_on,
        [resident(adapters.shape)],
        [adapters],
        cost_estimate=pl.CostEstimate(flops=HINT, bytes_accessed=0, transcendentals=0),
    )
    sibling = [(core, cores - 1 - core) for core in range(cores)]
    other_weight, other_adapters = (
        lax.ppermute(value, "c", sibling) for value in (projection_weight, adapters)
    )

    message_shape = resident((chips, groups, chip_width + LANES))
    state_shape = resident((groups, chip_width))
    message, wide, scale, held, weight, adapters = call(
        functools.partial(first_products, kept),
        [
            message_shape,
            state_shape,
            resident((1, chip_width), f32),
            resident((groups, LANES), i32),
            resident((chip_width, projection_weight.shape[1])),
            resident((2 * rank_cols, chip_width)),
        ],
        [got, other_weight, other_adapters, projection_weight, down, up, requests],
        far=4,
        scratch_shapes=[
            pltpu.VMEM(requests.shape, i32),
            pltpu.SemaphoreType.DMA((chips + 3,)),
        ],
    )
    message, state = call(
        functools.partial(next_products, kept),
        [message_shape, state_shape],
        [wide, exchange(message), held, scale, weight, adapters],
    )
    (back,) = call(
        functools.partial(last_update, kept),
        [resident((rows, DRAFT * width))],
        [state, exchange(message), held, adapters],
    )
    home = move(back.reshape(rows, DRAFT, width)).reshape(rows, DRAFT * width)
    (result,) = call(
        functools.partial(permute_out, kept),
        [jax.ShapeDtypeStruct((DRAFT, rows, width), bf16)],
        [requests, home],
    )
    return result


def solution(mesh):
    chip_mesh = Mesh(mesh.devices.reshape(mesh.shape["rep"], -1, 2), ("rep", "y", "c"))
    tp = ("y", "c")
    return jax.shard_map(
        shards,
        mesh=chip_mesh,
        in_specs=(
            P("rep", tp),
            P(tp),
            P(tp, None),
            P("rep", tp, None),
            P("rep", None, tp),
            P(),
        ),
        out_specs=P(None, "rep", tp),
        check_vma=False,
    )
```

```python
import functools

import jax
import jax.numpy as jnp
from jax import lax
from jax.experimental import pallas as pl
from jax.experimental.pallas import tpu as pltpu
from jax.sharding import Mesh, PartitionSpec as P

DRAFT = 2
LANES = 128
EPSILON = 1e-06
TURN = 46
TURN_Y = 2
HINT = 6 * 10**10
BANDS = 2
SLOT = 4

bf16, f32, i32 = jnp.bfloat16, jnp.float32, jnp.int32


def iota(shape, dim):
    return lax.broadcasted_iota(i32, shape, dim)


def over(values, size):
    return values >> (size.bit_length() - 1)


def within(values, size):
    return values & (size - 1)


def mm(left, right):
    return jnp.dot(left, right, preferred_element_type=f32)


def mm_t(left, right):
    return lax.dot_general(left, right, (((1,), (1,)), ((), ())), preferred_element_type=f32)


def t_mm(left, right):
    return lax.dot_general(left, right, (((0,), (0,)), ((), ())), preferred_element_type=f32)


def holder_places(my_requests, kept):
    blocks = my_requests.shape[1]
    return within(over(my_requests, kept) + (blocks - TURN), blocks)


def split(values):
    high = values.astype(bf16).astype(f32)
    middle = (values - high).astype(bf16).astype(f32)
    return high, middle, values - high - middle


def permute_in(kept, requests_hbm, x_hbm, scale_hbm, down_hbm, up_hbm, *refs):
    sent_ref, adapters_ref, requests_ref, x_ref, scale_ref, sems = refs
    rank_cols = down_hbm.shape[0]
    copies = [
        pltpu.make_async_copy(source, target, sems.at[index])
        for index, (source, target) in enumerate(
            (
                (x_hbm, x_ref),
                (requests_hbm, requests_ref),
                (scale_hbm, scale_ref),
                (down_hbm, adapters_ref.at[:rank_cols]),
                (up_hbm, adapters_ref.at[rank_cols:]),
            )
        )
    ]
    for copy in copies:
        copy.start()
    me = lax.axis_index("rep")
    blocks = requests_ref.shape[1]
    rows, width = x_ref.shape
    slots = sent_ref.shape[0]
    parts = width // LANES
    row_picks = jnp.concatenate(
        [
            (iota((blocks, rows), 1) == 2 * iota((blocks, rows), 0) + half).astype(bf16)
            for half in range(2)
        ]
    )
    piece = over(iota((1, 2 * parts * blocks), 1), blocks)
    slot = iota((slots, 2 * parts * blocks), 0) - jnp.where(piece < parts, piece, SLOT + piece - parts)
    padding = within(iota((slots, 1), 0), SLOT) == parts
    copies[2].wait()
    wanted = lax.rem(within(me + (blocks - TURN), blocks), 3 * parts)
    gain = jnp.zeros((1, LANES), f32)
    for part in range(parts):
        for number, value in enumerate(split(scale_ref[part : part + 1, :])):
            gain = jnp.where(wanted == 3 * part + number, value, gain)
    copies[1].wait()
    places = 2 * SLOT * holder_places(requests_ref[pl.ds(me, 1), :], kept)
    places = jnp.concatenate([jnp.concatenate([places, places], axis=1)] * parts, axis=1)
    lay_out = (slot == places).astype(bf16)
    copies[0].wait()
    halves = mm(row_picks, x_ref[...]).astype(bf16)
    stacked = jnp.concatenate(
        [
            halves[half * blocks : (half + 1) * blocks, part * LANES : (part + 1) * LANES]
            for half in range(2)
            for part in range(parts)
        ]
    )
    sent_ref[...] = jnp.where(padding, gain, mm(lay_out, stacked)).astype(bf16)
    for copy in copies[3:]:
        copy.wait()


def permute_out(kept, requests_ref, home_ref, out_ref):
    me = lax.axis_index("rep")
    blocks = requests_ref.shape[1]
    rows, width = out_ref.shape[1:]
    repeat = (over(iota((blocks, rows), 1), 2) == iota((blocks, rows), 0)).astype(bf16)
    places = holder_places(requests_ref[pl.ds(me, 1), :], kept)
    places = jnp.broadcast_to(places.astype(f32), (8, blocks)).astype(bf16)
    target = mm(places, repeat)[:1].astype(i32) * 2 + within(iota((1, rows), 1), 2)
    pick = (target == iota((rows, rows), 0)).astype(bf16)
    for step in range(DRAFT):
        out_ref[step] = t_mm(pick, home_ref[:, step * width : (step + 1) * width]).astype(bf16)


def unpack_picks(groups):
    slots, parts = 2 * SLOT * groups, SLOT - 1
    row, slot = iota((groups, slots), 0), iota((groups, slots), 1)
    picks = [
        (slot == (2 * row + core) * SLOT + part).astype(bf16)
        for core in range(2)
        for part in range(parts)
    ]
    row, slot = iota((16, slots), 0), iota((1, slots), 1)
    place, core = over(slot, 2 * SLOT), within(over(slot, SLOT), 2)
    part = (place >= 3).astype(i32) + (place >= 6).astype(i32)
    padding = (within(slot, SLOT) == parts) & (place < 3 * parts)
    picks.append((row == jnp.where(padding, core * parts + part, 16)).astype(bf16))
    return jnp.concatenate(picks)


def pass_on(value_ref, out_ref):
    out_ref[...] = value_ref[...]


def find_held(requests, kept):
    groups = requests.shape[0]
    mine = over(requests, kept) == lax.axis_index("rep")
    held = jnp.sum(jnp.where(mine, within(requests, kept), 0), axis=1, keepdims=True)
    held = jnp.broadcast_to(held.astype(f32), (groups, LANES)).astype(bf16)
    turn = within(iota((groups, groups), 0) + TURN, groups) == iota((groups, groups), 1)
    return mm(turn.astype(bf16), held).astype(i32)


def small_sums(wide, ranks, kept, held):
    count, rank_cols = ranks.shape
    rank = rank_cols // kept
    owned = over(iota((count, rank_cols), 1), rank) == held[:, :1]
    ranks = jnp.where(owned, ranks.astype(bf16), 0).astype(bf16)
    fold = within(iota((rank_cols, LANES), 0), rank) == iota((rank_cols, LANES), 1)
    sums = mm(ranks, fold.astype(bf16))
    squares = jnp.sum(wide * wide, axis=1, keepdims=True)
    top = squares.astype(bf16).astype(f32)
    lane = iota((count, LANES), 1)
    sums = jnp.where(lane == rank, top, sums)
    return jnp.where(lane == rank + 1, squares - top, sums).astype(bf16)


def update(wide, kept, held, got_ref, adapters):
    count, chip_width = wide.shape
    rank_cols = adapters.shape[0] // 2
    rank = rank_cols // kept
    chips = got_ref.shape[0]
    total = got_ref[0].astype(f32)
    for chip in range(1, chips):
        total += got_ref[chip].astype(f32)
    extra = total[:, chip_width:]
    lane = iota((count, LANES), 1)
    is_square = (lane == rank) | (lane == rank + 1)
    mean = jnp.sum(jnp.where(is_square, extra, 0.0), axis=1, keepdims=True) / (chip_width * chips)
    factor = lax.rsqrt(mean + EPSILON)
    ranks = jnp.where(lane < rank, extra * factor, 0.0).astype(bf16)
    unfold = within(iota((LANES, rank_cols), 1), rank) == iota((LANES, rank_cols), 0)
    spread = mm(ranks, unfold.astype(bf16))
    owned = over(iota((count, rank_cols), 1), rank) == held[:, :1]
    spread = jnp.where(owned, spread, 0.0).astype(bf16)
    delta = mm(spread, adapters[rank_cols:]).astype(bf16).astype(f32)
    return (wide + total[:, :chip_width] * factor + delta).astype(bf16)


def first_products(kept, x_ref, requests_ref, other_weight, others, own, weight_hbm, *refs):
    message_ref, wide_ref, scale_ref, held_ref, weight, adapters, sems = refs
    groups, chip_width = wide_ref.shape
    width = chip_width // 2
    rank_cols = adapters.shape[0] // 2
    chips = message_ref.shape[0]
    first = lax.axis_index("c") == 0
    my_place = pl.ds(pl.multiple_of(jnp.where(first, 0, width), LANES), width)
    other_place = pl.ds(pl.multiple_of(jnp.where(first, width, 0), LANES), width)
    columns = [pl.ds(chip * chip_width, chip_width) for chip in range(chips)]
    band = width // BANDS
    copies = [
        pltpu.make_async_copy(
            weight_hbm.at[pl.ds(index * band, band), :],
            weight.at[pl.ds(pl.multiple_of(jnp.where(first, 0, width) + index * band, 16), band), :],
            sems.at[index],
        )
        for index in range(BANDS)
    ]
    for copy in copies:
        copy.start()

    rows = mm(unpack_picks(groups), x_ref[...])
    parts = 2 * (SLOT - 1)
    wide = jnp.concatenate(
        [rows[index * groups : (index + 1) * groups] for index in range(parts)], axis=1
    )
    start = parts * groups
    scale = jnp.concatenate(
        [rows[start + index : start + index + 1] for index in range(parts)], axis=1
    )
    wide_ref[...] = wide.astype(bf16)
    scale_ref[...] = scale
    scaled = (wide * scale).astype(bf16)
    low, high = scaled[:, :width], scaled[:, width:]
    mine, other = jnp.where(first, low, high), jnp.where(first, high, low)
    sums = [mm(other, other_weight[:, cols]) for cols in columns]
    held = find_held(requests_ref[...], kept)
    held_ref[...] = held
    ranks = mm_t(mine, own[:rank_cols]) + mm_t(other, others[:rank_cols])
    small = small_sums(wide, ranks, kept, held)
    adapters[:, my_place] = own[...]
    adapters[:, other_place] = others[...]
    for cols in columns:
        weight[other_place, cols] = other_weight[:, cols]
    for copy in copies:
        copy.wait()
    for chip, cols in enumerate(columns):
        place = within(chip + chips - TURN_Y, chips)
        product = sums[chip] + mm(mine, weight[my_place, cols])
        message_ref[place, :, :chip_width] = product.astype(bf16)
        message_ref[place, :, chip_width:] = small


def next_products(kept, wide_ref, got_ref, held_ref, scale_ref, weight, adapters, *refs):
    message_ref, state_ref = refs
    held = held_ref[...]
    state = update(wide_ref[...].astype(f32), kept, held, got_ref, adapters)
    state_ref[...] = state
    chips = message_ref.shape[0]
    chip_width = state.shape[1]
    wide = state.astype(f32)
    scaled = (wide * scale_ref[...]).astype(bf16)
    ranks = mm_t(scaled, adapters[: adapters.shape[0] // 2])
    small = small_sums(wide, ranks, kept, held)
    for chip in range(chips):
        place = within(chip + chips - TURN_Y, chips)
        message_ref[place, :, :chip_width] = mm(
            scaled, weight[:, chip * chip_width : (chip + 1) * chip_width]
        ).astype(bf16)
        message_ref[place, :, chip_width:] = small


def last_update(kept, state_ref, got_ref, held_ref, adapters, back_ref):
    rows, cols = back_ref.shape
    width = cols // DRAFT
    old = state_ref[...]
    new = update(old.astype(f32), kept, held_ref[...], got_ref, adapters)
    row, place = iota((rows // 2, rows), 0), iota((rows // 2, rows), 1)
    picks = [(place == 2 * row + core).astype(bf16) for core in range(2)]
    for step, state in enumerate((old, new)):
        back_ref[:, step * width : (step + 1) * width] = sum(
            t_mm(pick, state[:, core * width : (core + 1) * width])
            for core, pick in enumerate(picks)
        ).astype(bf16)


def call(kernel, outs, operands, far=0, **kwargs):
    spaces = [pltpu.VMEM] * (len(operands) - far) + [pltpu.HBM] * far
    return pl.pallas_call(
        kernel,
        out_shape=outs,
        in_specs=[pl.BlockSpec(memory_space=space) for space in spaces],
        out_specs=[
            pl.BlockSpec(memory_space=getattr(out, "memory_space", pltpu.VMEM)) for out in outs
        ],
        compiler_params=pltpu.CompilerParams(vmem_limit_bytes=24 * 2**20),
        **kwargs,
    )(*map(pltpu.with_memory_space_constraint, operands, spaces))


def shards(first_hidden_rows, norm_scale, projection_weight, down_weights, up_weights, requests):
    groups = lax.axis_size("rep")
    chips = lax.axis_size("y")
    cores = lax.axis_size("c")
    rows, width = first_hidden_rows.shape
    chip_width = width * cores
    kept, _, rank = down_weights.shape
    rank_cols = kept * rank

    def resident(shape, dtype=bf16):
        return pltpu.VMEM(shape, dtype)

    down = jnp.transpose(down_weights, (0, 2, 1)).reshape(rank_cols, width)
    up = up_weights.reshape(rank_cols, width)
    sent, adapters, near_requests = call(
        functools.partial(permute_in, kept),
        [
            resident((SLOT * rows, LANES)),
            resident((2 * rank_cols, width)),
            resident(requests.shape, i32),
        ],
        [requests, first_hidden_rows, norm_scale.reshape(-1, LANES), down, up],
        far=5,
        scratch_shapes=[
            pltpu.VMEM((rows, width), bf16),
            pltpu.VMEM((width // LANES, LANES), f32),
            pltpu.SemaphoreType.DMA((5,)),
        ],
    )
    movers = [[(place + TURN * cores) % rows for place in range(rows)]]
    adders = [[(place + TURN_Y) % chips for place in range(chips)]]

    def move(value):
        return lax.all_to_all(
            value, ("rep", "c"), split_axis=0, concat_axis=0, axis_index_groups=movers, tiled=True
        )

    def exchange(message):
        return lax.all_to_all(
            message, "y", split_axis=0, concat_axis=0, axis_index_groups=adders, tiled=True
        )

    got = move(sent.reshape(rows, SLOT, LANES)).reshape(SLOT * rows, LANES)

    (adapters,) = call(
        pass_on,
        [resident(adapters.shape)],
        [adapters],
        cost_estimate=pl.CostEstimate(flops=HINT, bytes_accessed=0, transcendentals=0),
    )
    sibling = [(core, cores - 1 - core) for core in range(cores)]
    other_weight, other_adapters = (
        lax.ppermute(value, "c", sibling) for value in (projection_weight, adapters)
    )

    message_shape = resident((chips, groups, chip_width + LANES))
    state_shape = resident((groups, chip_width))
    message, wide, scale, held, weight, adapters = call(
        functools.partial(first_products, kept),
        [
            message_shape,
            state_shape,
            resident((1, chip_width), f32),
            resident((groups, LANES), i32),
            resident((chip_width, projection_weight.shape[1])),
            resident((2 * rank_cols, chip_width)),
        ],
        [got, near_requests, other_weight, other_adapters, adapters, projection_weight],
        far=1,
        scratch_shapes=[pltpu.SemaphoreType.DMA((BANDS,))],
    )
    message, state = call(
        functools.partial(next_products, kept),
        [message_shape, state_shape],
        [wide, exchange(message), held, scale, weight, adapters],
    )
    (back,) = call(
        functools.partial(last_update, kept),
        [resident((rows, DRAFT * width))],
        [state, exchange(message), held, adapters],
    )
    home = move(back.reshape(rows, DRAFT, width)).reshape(rows, DRAFT * width)
    (result,) = call(
        functools.partial(permute_out, kept),
        [jax.ShapeDtypeStruct((DRAFT, rows, width), bf16)],
        [requests, home],
    )
    return result


def solution(mesh):
    chip_mesh = Mesh(mesh.devices.reshape(mesh.shape["rep"], -1, 2), ("rep", "y", "c"))
    tp = ("y", "c")
    return jax.shard_map(
        shards,
        mesh=chip_mesh,
        in_specs=(
            P("rep", tp),
            P(tp),
            P(tp, None),
            P("rep", tp, None),
            P("rep", None, tp),
            P(),
        ),
        out_specs=P(None, "rep", tp),
        check_vma=False,
    )
```

```python
import functools

import jax
import jax.numpy as jnp
from jax import lax
from jax.experimental import pallas as pl
from jax.experimental.pallas import tpu as pltpu
from jax.sharding import Mesh, PartitionSpec as P

DRAFT = 2
LANES = 128
EPSILON = 1e-06
TURN = 46
TURN_Y = 2
HINT = 6 * 10**10
SLOT = 4

bf16, f32, i32 = jnp.bfloat16, jnp.float32, jnp.int32


def iota(shape, dim):
    return lax.broadcasted_iota(i32, shape, dim)


def over(values, size):
    return values >> (size.bit_length() - 1)


def within(values, size):
    return values & (size - 1)


def mm(left, right):
    return jnp.dot(left, right, preferred_element_type=f32)


def mm_t(left, right):
    return lax.dot_general(left, right, (((1,), (1,)), ((), ())), preferred_element_type=f32)


def t_mm(left, right):
    return lax.dot_general(left, right, (((0,), (0,)), ((), ())), preferred_element_type=f32)


def holder_places(my_requests, kept):
    blocks = my_requests.shape[1]
    return within(over(my_requests, kept) + (blocks - TURN), blocks)


def split(values):
    high = values.astype(bf16).astype(f32)
    middle = (values - high).astype(bf16).astype(f32)
    return high, middle, values - high - middle


def permute_in(kept, requests_hbm, x_hbm, scale_hbm, sent_ref, requests_ref, x_ref, scale_ref, sems):
    copies = [
        pltpu.make_async_copy(source, target, sems.at[index])
        for index, (source, target) in enumerate(
            (
                (x_hbm, x_ref),
                (requests_hbm, requests_ref),
                (scale_hbm, scale_ref),
            )
        )
    ]
    for copy in copies:
        copy.start()
    me = lax.axis_index("rep")
    blocks = requests_ref.shape[1]
    rows, width = x_ref.shape
    slots = sent_ref.shape[0]
    parts = width // LANES
    row_picks = jnp.concatenate(
        [
            (iota((blocks, rows), 1) == 2 * iota((blocks, rows), 0) + half).astype(bf16)
            for half in range(2)
        ]
    )
    piece = over(iota((1, 2 * parts * blocks), 1), blocks)
    slot = iota((slots, 2 * parts * blocks), 0) - jnp.where(piece < parts, piece, SLOT + piece - parts)
    padding = within(iota((slots, 1), 0), SLOT) == parts
    copies[2].wait()
    wanted = lax.rem(within(me + (blocks - TURN), blocks), 3 * parts)
    gain = jnp.zeros((1, LANES), f32)
    for part in range(parts):
        for number, value in enumerate(split(scale_ref[part : part + 1, :])):
            gain = jnp.where(wanted == 3 * part + number, value, gain)
    copies[1].wait()
    places = 2 * SLOT * holder_places(requests_ref[pl.ds(me, 1), :], kept)
    places = jnp.concatenate([jnp.concatenate([places, places], axis=1)] * parts, axis=1)
    lay_out = (slot == places).astype(bf16)
    copies[0].wait()
    halves = mm(row_picks, x_ref[...]).astype(bf16)
    stacked = jnp.concatenate(
        [
            halves[half * blocks : (half + 1) * blocks, part * LANES : (part + 1) * LANES]
            for half in range(2)
            for part in range(parts)
        ]
    )
    sent_ref[...] = jnp.where(padding, gain, mm(lay_out, stacked)).astype(bf16)


def permute_out(kept, requests_ref, home_ref, out_ref):
    me = lax.axis_index("rep")
    blocks = requests_ref.shape[1]
    rows, width = out_ref.shape[1:]
    repeat = (over(iota((blocks, rows), 1), 2) == iota((blocks, rows), 0)).astype(bf16)
    places = holder_places(requests_ref[pl.ds(me, 1), :], kept)
    places = jnp.broadcast_to(places.astype(f32), (8, blocks)).astype(bf16)
    target = mm(places, repeat)[:1].astype(i32) * 2 + within(iota((1, rows), 1), 2)
    pick = (target == iota((rows, rows), 0)).astype(bf16)
    for step in range(DRAFT):
        out_ref[step] = t_mm(pick, home_ref[:, step * width : (step + 1) * width]).astype(bf16)


def unpack_picks(groups):
    slots, parts = 2 * SLOT * groups, SLOT - 1
    row, slot = iota((groups, slots), 0), iota((groups, slots), 1)
    picks = [
        (slot == (2 * row + core) * SLOT + part).astype(bf16)
        for core in range(2)
        for part in range(parts)
    ]
    row, slot = iota((16, slots), 0), iota((1, slots), 1)
    place, core = over(slot, 2 * SLOT), within(over(slot, SLOT), 2)
    part = (place >= 3).astype(i32) + (place >= 6).astype(i32)
    padding = (within(slot, SLOT) == parts) & (place < 3 * parts)
    picks.append((row == jnp.where(padding, core * parts + part, 16)).astype(bf16))
    return jnp.concatenate(picks)


def pack(down_hbm, up_hbm, out_ref, sems):
    rank_cols = down_hbm.shape[0]
    copies = [
        pltpu.make_async_copy(down_hbm, out_ref.at[:rank_cols], sems.at[0]),
        pltpu.make_async_copy(up_hbm, out_ref.at[rank_cols:], sems.at[1]),
    ]
    for copy in copies:
        copy.start()
    for copy in copies:
        copy.wait()


def find_held(requests, kept):
    groups = requests.shape[0]
    mine = over(requests, kept) == lax.axis_index("rep")
    held = jnp.sum(jnp.where(mine, within(requests, kept), 0), axis=1, keepdims=True)
    held = jnp.broadcast_to(held.astype(f32), (groups, LANES)).astype(bf16)
    turn = within(iota((groups, groups), 0) + TURN, groups) == iota((groups, groups), 1)
    return mm(turn.astype(bf16), held).astype(i32)


def small_sums(wide, ranks, kept, held):
    count, rank_cols = ranks.shape
    rank = rank_cols // kept
    owned = over(iota((count, rank_cols), 1), rank) == held[:, :1]
    ranks = jnp.where(owned, ranks.astype(bf16), 0).astype(bf16)
    fold = within(iota((rank_cols, LANES), 0), rank) == iota((rank_cols, LANES), 1)
    sums = mm(ranks, fold.astype(bf16))
    squares = jnp.sum(wide * wide, axis=1, keepdims=True)
    top = squares.astype(bf16).astype(f32)
    lane = iota((count, LANES), 1)
    sums = jnp.where(lane == rank, top, sums)
    return jnp.where(lane == rank + 1, squares - top, sums).astype(bf16)


def update(wide, kept, held, got_ref, adapters):
    count, chip_width = wide.shape
    rank_cols = adapters.shape[0] // 2
    rank = rank_cols // kept
    chips = got_ref.shape[0]
    total = got_ref[0].astype(f32)
    for chip in range(1, chips):
        total += got_ref[chip].astype(f32)
    extra = total[:, chip_width:]
    lane = iota((count, LANES), 1)
    is_square = (lane == rank) | (lane == rank + 1)
    mean = jnp.sum(jnp.where(is_square, extra, 0.0), axis=1, keepdims=True) / (chip_width * chips)
    factor = lax.rsqrt(mean + EPSILON)
    ranks = jnp.where(lane < rank, extra * factor, 0.0).astype(bf16)
    unfold = within(iota((LANES, rank_cols), 1), rank) == iota((LANES, rank_cols), 0)
    spread = mm(ranks, unfold.astype(bf16))
    owned = over(iota((count, rank_cols), 1), rank) == held[:, :1]
    spread = jnp.where(owned, spread, 0.0).astype(bf16)
    delta = mm(spread, adapters[rank_cols:]).astype(bf16).astype(f32)
    return (wide + total[:, :chip_width] * factor + delta).astype(bf16)


def first_products(kept, x_ref, requests_ref, other_weight, others, own, weight_hbm, *refs):
    message_ref, wide_ref, scale_ref, held_ref, weight, adapters, sems = refs
    groups, chip_width = wide_ref.shape
    width = chip_width // 2
    rank_cols = adapters.shape[0] // 2
    chips = message_ref.shape[0]
    first = lax.axis_index("c") == 0
    my_place = pl.ds(pl.multiple_of(jnp.where(first, 0, width), LANES), width)
    other_place = pl.ds(pl.multiple_of(jnp.where(first, width, 0), LANES), width)
    columns = [pl.ds(chip * chip_width, chip_width) for chip in range(chips)]
    half = chips // 2 * chip_width
    copies = [
        pltpu.make_async_copy(
            weight_hbm.at[:, pl.ds(start, half)],
            weight.at[my_place, pl.ds(start, half)],
            sems.at[start // half],
        )
        for start in (0, half)
    ]
    copies[0].start()

    rows = mm(unpack_picks(groups), x_ref[...])
    parts = 2 * (SLOT - 1)
    wide = jnp.concatenate(
        [rows[index * groups : (index + 1) * groups] for index in range(parts)], axis=1
    )
    start = parts * groups
    scale = jnp.concatenate(
        [rows[start + index : start + index + 1] for index in range(parts)], axis=1
    )
    wide_ref[...] = wide.astype(bf16)
    scale_ref[...] = scale
    scaled = (wide * scale).astype(bf16)
    low, high = scaled[:, :width], scaled[:, width:]
    mine, other = jnp.where(first, low, high), jnp.where(first, high, low)
    sums = [mm(other, other_weight[:, cols]) for cols in columns]
    held = find_held(requests_ref[...], kept)
    held_ref[...] = held
    ranks = mm_t(mine, own[:rank_cols]) + mm_t(other, others[:rank_cols])
    small = small_sums(wide, ranks, kept, held)
    adapters[:, my_place] = own[...]
    adapters[:, other_place] = others[...]
    for cols in columns:
        weight[other_place, cols] = other_weight[:, cols]
    copies[1].start()
    for chip, cols in enumerate(columns):
        place = within(chip + chips - TURN_Y, chips)
        if chip % (chips // 2) == 0:
            copies[chip * 2 // chips].wait()
        product = sums[chip] + mm(mine, weight[my_place, cols])
        message_ref[place, :, :chip_width] = product.astype(bf16)
        message_ref[place, :, chip_width:] = small


def next_products(kept, wide_ref, got_ref, held_ref, scale_ref, weight, adapters, *refs):
    message_ref, state_ref = refs
    held = held_ref[...]
    state = update(wide_ref[...].astype(f32), kept, held, got_ref, adapters)
    state_ref[...] = state
    chips = message_ref.shape[0]
    chip_width = state.shape[1]
    wide = state.astype(f32)
    scaled = (wide * scale_ref[...]).astype(bf16)
    ranks = mm_t(scaled, adapters[: adapters.shape[0] // 2])
    small = small_sums(wide, ranks, kept, held)
    for chip in range(chips):
        place = within(chip + chips - TURN_Y, chips)
        message_ref[place, :, :chip_width] = mm(
            scaled, weight[:, chip * chip_width : (chip + 1) * chip_width]
        ).astype(bf16)
        message_ref[place, :, chip_width:] = small


def last_update(kept, state_ref, got_ref, held_ref, adapters, back_ref):
    rows, cols = back_ref.shape
    width = cols // DRAFT
    old = state_ref[...]
    new = update(old.astype(f32), kept, held_ref[...], got_ref, adapters)
    row, place = iota((rows // 2, rows), 0), iota((rows // 2, rows), 1)
    picks = [(place == 2 * row + core).astype(bf16) for core in range(2)]
    for step, state in enumerate((old, new)):
        back_ref[:, step * width : (step + 1) * width] = sum(
            t_mm(pick, state[:, core * width : (core + 1) * width])
            for core, pick in enumerate(picks)
        ).astype(bf16)


def call(kernel, outs, operands, far=0, **kwargs):
    spaces = [pltpu.VMEM] * (len(operands) - far) + [pltpu.HBM] * far
    return pl.pallas_call(
        kernel,
        out_shape=outs,
        in_specs=[pl.BlockSpec(memory_space=space) for space in spaces],
        out_specs=[
            pl.BlockSpec(memory_space=getattr(out, "memory_space", pltpu.VMEM)) for out in outs
        ],
        compiler_params=pltpu.CompilerParams(vmem_limit_bytes=24 * 2**20),
        **kwargs,
    )(*map(pltpu.with_memory_space_constraint, operands, spaces))


def shards(first_hidden_rows, norm_scale, projection_weight, down_weights, up_weights, requests):
    groups = lax.axis_size("rep")
    chips = lax.axis_size("y")
    cores = lax.axis_size("c")
    rows, width = first_hidden_rows.shape
    chip_width = width * cores
    kept, _, rank = down_weights.shape
    rank_cols = kept * rank

    def resident(shape, dtype=bf16):
        return pltpu.VMEM(shape, dtype)

    down = jnp.transpose(down_weights, (0, 2, 1)).reshape(rank_cols, width)
    up = up_weights.reshape(rank_cols, width)
    sent, near_requests = call(
        functools.partial(permute_in, kept),
        [
            resident((SLOT * rows, LANES)),
            resident(requests.shape, i32),
        ],
        [requests, first_hidden_rows, norm_scale.reshape(-1, LANES)],
        far=3,
        scratch_shapes=[
            pltpu.VMEM((rows, width), bf16),
            pltpu.VMEM((width // LANES, LANES), f32),
            pltpu.SemaphoreType.DMA((3,)),
        ],
    )
    movers = [[(place + TURN * cores) % rows for place in range(rows)]]
    adders = [[(place + TURN_Y) % chips for place in range(chips)]]

    def move(value):
        return lax.all_to_all(
            value, ("rep", "c"), split_axis=0, concat_axis=0, axis_index_groups=movers, tiled=True
        )

    def exchange(message):
        return lax.all_to_all(
            message, "y", split_axis=0, concat_axis=0, axis_index_groups=adders, tiled=True
        )

    got = move(sent.reshape(rows, SLOT, LANES)).reshape(SLOT * rows, LANES)

    (adapters,) = call(
        pack,
        [resident((2 * rank_cols, width))],
        [down, up],
        far=2,
        scratch_shapes=[pltpu.SemaphoreType.DMA((2,))],
        cost_estimate=pl.CostEstimate(flops=HINT, bytes_accessed=0, transcendentals=0),
    )
    sibling = [(core, cores - 1 - core) for core in range(cores)]
    other_weight, other_adapters = (
        lax.ppermute(value, "c", sibling) for value in (projection_weight, adapters)
    )

    message_shape = resident((chips, groups, chip_width + LANES))
    state_shape = resident((groups, chip_width))
    message, wide, scale, held, weight, adapters = call(
        functools.partial(first_products, kept),
        [
            message_shape,
            state_shape,
            resident((1, chip_width), f32),
            resident((groups, LANES), i32),
            resident((chip_width, projection_weight.shape[1])),
            resident((2 * rank_cols, chip_width)),
        ],
        [got, near_requests, other_weight, other_adapters, adapters, projection_weight],
        far=1,
        scratch_shapes=[pltpu.SemaphoreType.DMA((2,))],
    )
    message, state = call(
        functools.partial(next_products, kept),
        [message_shape, state_shape],
        [wide, exchange(message), held, scale, weight, adapters],
    )
    (back,) = call(
        functools.partial(last_update, kept),
        [resident((rows, DRAFT * width))],
        [state, exchange(message), held, adapters],
    )
    home = move(back.reshape(rows, DRAFT, width)).reshape(rows, DRAFT * width)
    (result,) = call(
        functools.partial(permute_out, kept),
        [jax.ShapeDtypeStruct((DRAFT, rows, width), bf16)],
        [requests, home],
    )
    return result


def solution(mesh):
    chip_mesh = Mesh(mesh.devices.reshape(mesh.shape["rep"], -1, 2), ("rep", "y", "c"))
    tp = ("y", "c")
    return jax.shard_map(
        shards,
        mesh=chip_mesh,
        in_specs=(
            P("rep", tp),
            P(tp),
            P(tp, None),
            P("rep", tp, None),
            P("rep", None, tp),
            P(),
        ),
        out_specs=P(None, "rep", tp),
        check_vma=False,
    )
```
